32 devices in a mesh: row: 4 (over y, x), col: 8 (over z, core).
Axes of the slice: x: 2, y: 2, z: 4, core: 2. Of those that a mesh axis runs over, the one named last changes fastest.
Arguments:
- local_ops: bfloat16 [4, 8, 2048, 2048], P('row', 'col'), may hold values from -2 to 30, as said below
- loads: float32 [4, 8, 2048, 256], P('row', 'col'), may hold values from -6 to 6
- modes: float32 [4, 8, 32, 2048], P('row', 'col'), may hold values from -1 to 1
- coarse_inverse: float32 [1024, 1024], P('row', 'col'), may hold values from -1 to 1
- face_rows: int32 [4, 8, 4, 512], P('row', 'col'), may hold values from 0 to 2047, as said below
- adjacency: int32 [4, 8, 4], P('row', 'col'), may hold values from 0 to 1, as said below
- contact: int32 [4, 8, 2048], P('row', 'col'), may hold values 0 or 1
Outputs:
- multipliers: float32 [4, 8, 2048, 256], P('row', 'col')
The draws below stay inside these ranges and needn't reach their ends.
Inputs may be any that keep to these rules, and one draw needn't show every extreme that they name: `face_rows`: for each subdomain the 2048 entries are a permutation of 0 to 2047. `adjacency`: symmetric across each shared face (a subdomain's south flag equals the north flag of the one below it, its east flag the west flag of the one to its right); 0 on faces at the grid's edge. `local_ops`: each subdomain's local dual operator is symmetric positive definite.
All inputs are finite; a program needn't handle non-finite values. No bound on the sum of `contact` on one device may be relied on, other than what follows from the above.
Results may differ from the reference program's by a relative error of at most 0.00099.
Values sent between devices are 32-bit elements; how exact they have to be, the bound alone decides.
No kernel may reach another device: no remote copies, remote signals or barrier semaphores. Data moves between devices by JAX's collectives and lax.ppermute only.
A program may use at most 128 MiB of HBM per device.

```python
import jax
import jax.numpy as jnp
from jax import lax

M = 2048
NM = 32
K = 256
ITERS = 2
FACE = 512
GRID_ROWS = 4
GRID_COLS = 8
NCO = 1024


def draw_local_ops(key, part):
    subdomains = GRID_ROWS * GRID_COLS
    base_key = jax.random.fold_in(key, 101)

    def draw_one(position):
        sub_key = jax.random.fold_in(base_key, position)
        first_key, second_key = jax.random.split(sub_key)
        ratio = position.astype(jnp.float32) / max(subdomains - 1, 1)
        factor = 3.0 ** ratio
        noise_part = jnp.clip(jax.random.normal(first_key, (M, M), jnp.float32), -4.0, 4.0)
        symmetric = (noise_part + noise_part.T) * 0.70710678
        diagonal = jnp.exp(jax.random.uniform(second_key, (M,), jnp.float32, jnp.log(1.2), jnp.log(3.0)))
        matrix = factor * (0.45 / M ** 0.5 * symmetric + jnp.diag(diagonal))
        return matrix.astype(jnp.bfloat16)
    stacked = lax.map(draw_one, jnp.arange(subdomains, dtype=jnp.int32))
    return stacked.reshape(GRID_ROWS, GRID_COLS, M, M)


def draw_coarse_inverse(key, part):
    sub_key = jax.random.fold_in(key, 202)
    noise_part = jnp.clip(jax.random.normal(sub_key, (NCO, NCO), jnp.float32), -4.0, 4.0)
    scale_value = 0.5 * (NM / M) ** 0.5
    return scale_value * (jnp.eye(NCO, dtype=jnp.float32) + 0.6 * noise_part / NCO ** 0.5)


def draw_face_rows(key, part):
    key_list = jax.random.split(jax.random.fold_in(key, 303), GRID_ROWS * GRID_COLS)

    def permute_one(sub_key):
        return jax.random.permutation(sub_key, M).astype(jnp.int32)
    permuted = jax.vmap(permute_one)(key_list)
    return permuted.reshape(GRID_ROWS, GRID_COLS, 4, FACE).astype(jnp.int32)


def draw_adjacency(key, part):
    first_key, second_key = jax.random.split(jax.random.fold_in(key, 404))
    vertical = (jax.random.randint(first_key, (GRID_ROWS, GRID_COLS), 0, 4) < 3).astype(jnp.int32)
    lateral = (jax.random.randint(second_key, (GRID_ROWS, GRID_COLS), 0, 4) < 3).astype(jnp.int32)
    vertical = vertical.at[GRID_ROWS - 1, :].set(0)
    lateral = lateral.at[:, GRID_COLS - 1].set(0)
    north = jnp.concatenate([jnp.zeros((1, GRID_COLS), jnp.int32), vertical[:-1]], axis=0)
    west = jnp.concatenate([jnp.zeros((GRID_ROWS, 1), jnp.int32), lateral[:, :-1]], axis=1)
    return jnp.stack([north, vertical, west, lateral], axis=-1).astype(jnp.int32)


def set_ends(drawn, rng, least, high):
    place = [jax.random.randint(jax.random.fold_in(rng, axis), (), 0, length) for axis, length in enumerate(drawn.shape)]
    main_axis = drawn.shape.index(max(drawn.shape))
    neighbour = place[:main_axis] + [(place[main_axis] + 1) % drawn.shape[main_axis]] + place[main_axis + 1:]
    return drawn.at[tuple(place)].set(least).at[tuple(neighbour)].set(high)


def steps_of(own_key, extent, cuts, low, largest):
    def one(dim, shards_of):
        heights = jax.random.uniform(jax.random.fold_in(jax.random.fold_in(own_key, 6), dim), (shards_of,), jnp.float32, low / len(cuts), largest / len(cuts))
        return jnp.repeat(jnp.exp(heights), extent[dim] // shards_of).reshape((-1,) + (1,) * (len(extent) - dim - 1))

    loudness = one(*cuts[0])
    for cut in cuts[1:]:
        loudness = loudness * one(*cut)
    return loudness


def normal_values(rng, extent, spread, bound, cuts=(), held_as=jnp.bfloat16):
    loudness = steps_of(rng, extent, cuts, -0.22, 0.18) if cuts else 1.0
    drawn = jax.random.normal(rng, extent, jnp.float32) * spread * loudness
    return jnp.minimum(jnp.maximum(drawn, -bound), bound).astype(held_as)


def setup_inputs(seed: int = 0) -> dict:
    keys = jax.random.split(jax.random.key(seed), 8)
    return {
        "local_ops": draw_local_ops(jax.random.fold_in(keys[7], 71), 0),
        "loads": normal_values(keys[1], (GRID_ROWS, GRID_COLS, M, K), 1.0, 6.0, ((0, 4), (1, 8)), jnp.float32),
        "modes": normal_values(keys[2], (GRID_ROWS, GRID_COLS, NM, M), NM ** -0.5, 1.0, ((0, 4), (1, 8)), jnp.float32),
        "coarse_inverse": draw_coarse_inverse(jax.random.fold_in(keys[7], 71), 0),
        "face_rows": draw_face_rows(jax.random.fold_in(keys[7], 71), 0),
        "adjacency": draw_adjacency(jax.random.fold_in(keys[7], 71), 0),
        "contact": set_ends((jax.random.randint(keys[6], (GRID_ROWS, GRID_COLS, M), 0, 2) < 1).astype(jnp.int32), jax.random.fold_in(keys[6], 1), 0, 1),
    }


def face_blocks(field_values, face_rows):
    def pick_rows(values, indices):
        return values[indices]
    return jax.vmap(jax.vmap(pick_rows))(field_values, face_rows)


def assemble(field_values, face_rows, adj_flags):
    blocks = face_blocks(field_values, face_rows)
    zero_row = jnp.zeros_like(blocks[:1, :, 0])
    north = jnp.concatenate([zero_row, blocks[:-1, :, 1]], axis=0)
    south = jnp.concatenate([blocks[1:, :, 0], zero_row], axis=0)
    zero_col = jnp.zeros_like(blocks[:, :1, 2])
    west = jnp.concatenate([zero_col, blocks[:, :-1, 3]], axis=1)
    east = jnp.concatenate([blocks[:, 1:, 2], zero_col], axis=1)
    incoming = jnp.stack([north, south, west, east], axis=2) * adj_flags[:, :, :, None, None]

    def add_rows(values, indices, incoming_rows):
        return values.at[indices.reshape(-1)].add(incoming_rows.reshape(-1, incoming_rows.shape[-1]))
    return jax.vmap(jax.vmap(add_rows))(field_values, face_rows, incoming)


def apply_ops(local_ops, field_values):
    grid_rows, grid_cols, order, _ = local_ops.shape
    flat_ops = local_ops.reshape(grid_rows * grid_cols, order, order)
    flat_vec = field_values.astype(jnp.bfloat16).reshape(grid_rows * grid_cols, order, -1)

    def product(operands):
        return jnp.dot(operands[0], operands[1], preferred_element_type=jnp.float32)
    return lax.map(product, (flat_ops, flat_vec)).reshape(field_values.shape)


def reference(local_ops, loads, modes, coarse_inverse, face_rows, adjacency, contact):
    adj_flags = adjacency.astype(jnp.float32)
    face_size = face_rows.shape[-1]
    free_face = jnp.repeat(1.0 - adj_flags, face_size, axis=-1)

    def place_values(indices, values):
        return jnp.zeros((loads.shape[2],), jnp.float32).at[indices.reshape(-1)].set(values)
    row_free = jax.vmap(jax.vmap(place_values))(face_rows, free_face)
    weight = 0.5 + 0.5 * row_free
    clamp_rows = contact.astype(jnp.float32) * row_free > 0.5
    multipliers = jnp.zeros(loads.shape, jnp.float32)
    for iteration in range(ITERS):
        if iteration == 0:
            local_term = -loads
        else:
            local_term = apply_ops(local_ops, multipliers) - loads
        gradient = assemble(local_term, face_rows, adj_flags)
        coarse_coef = jnp.einsum("abmr,abrk->abmk", modes, gradient, precision=lax.Precision.HIGHEST)
        case_count = coarse_coef.shape[-1]
        coarse_amount = jnp.dot(coarse_inverse, coarse_coef.reshape(-1, case_count), precision=lax.Precision.HIGHEST, preferred_element_type=jnp.float32).reshape(coarse_coef.shape)
        correction = jnp.einsum("abmr,abmk->abrk", modes, coarse_amount, precision=lax.Precision.HIGHEST)
        direction = gradient - assemble(correction, face_rows, adj_flags)
        operated = apply_ops(local_ops, direction)
        numerator = jnp.sum(weight[..., None] * direction * direction, axis=(0, 1, 2))
        denominator = jnp.sum(direction * operated, axis=(0, 1, 2))
        step_length = numerator / denominator
        multipliers = multipliers - step_length * direction
        multipliers = jnp.where(clamp_rows[..., None], jnp.maximum(multipliers, 0.0), multipliers)
    return multipliers
```

```python
import functools

import jax
import jax.numpy as jnp
from jax import lax
from jax.experimental import pallas as pl
from jax.experimental.pallas import tpu as pltpu
from jax.sharding import PartitionSpec as P

F32 = jnp.float32
BF16 = jnp.bfloat16
PAD = 8
MIB = 1024 * 1024
VMEM = pl.BlockSpec(memory_space=pltpu.VMEM)
SMEM = pl.BlockSpec(memory_space=pltpu.SMEM)
HBM = pl.BlockSpec(memory_space=pltpu.HBM)


def dot(a, b):
    return lax.dot_general(a, b, (((1,), (0,)), ((), ())), preferred_element_type=F32)


def dot_nt(a, b):
    return lax.dot_general(a, b, (((1,), (1,)), ((), ())), preferred_element_type=F32)


def parts_of(x):
    high = x.astype(BF16)
    return high, (x - high.astype(F32)).astype(BF16)


def dot3(a, b):
    return dot(a[0], b[0]) + (dot(a[0], b[1]) + dot(a[1], b[0]))


def column_of(row, lanes=128):
    return jnp.transpose(jnp.broadcast_to(row, (lanes, row.shape[1])))[:, :1]


def tile_rows(i, tile):
    return pl.ds(pl.multiple_of(i * tile, tile), tile)


def total_of(refs):
    value = refs[0][...]
    for ref in refs[1:]:
        value = value + ref[...]
    return value


def call(kernel, name, args, in_specs, outs, scratch, grant, flops):
    moved = sum(x.size * x.dtype.itemsize for x in args)
    return pl.pallas_call(
        kernel,
        in_specs=in_specs,
        out_specs=[VMEM] * len(outs),
        out_shape=outs,
        scratch_shapes=scratch,
        compiler_params=pltpu.CompilerParams(vmem_limit_bytes=grant * MIB),
        cost_estimate=pl.CostEstimate(flops=int(flops), bytes_accessed=int(moved), transcendentals=0),
        name=name,
    )(*args)


def in_hbm(x):
    return pltpu.with_memory_space_constraint(x, pltpu.HBM)


def in_vmem(arrays):
    return [pltpu.with_memory_space_constraint(x, pltpu.VMEM) for x in arrays]


def shaped(shape, dtype=F32):
    return pltpu.VMEM(shape, dtype)


def pair_face(base, index):
    return base + 1 - index % 2


def cross_face(base, index):
    return base + index % 2


def face_kernel(base, with_modes, place_ref, rows_ref, *refs):
    if base:
        x_parts, *refs = refs
        if with_modes:
            m_parts, *refs = refs
        outs = refs
    elif with_modes:
        sources, refs = refs[:2], refs[2:]
        *outs, x_parts, m_parts, x_ref, modes_ref, sems = refs
        copies = [
            pltpu.make_async_copy(source, held, sems.at[k])
            for k, (source, held) in enumerate(zip(sources, (x_ref, modes_ref)))
        ]
        for copy in copies:
            copy.start()
        for copy in copies:
            copy.wait()
        high, low = parts_of(modes_ref[...])
        count = modes_ref.shape[0]
        m_parts[:count] = high
        m_parts[count:] = low
    else:
        x_ref, *outs, x_parts = refs
    order, cases = x_parts.shape[0], x_parts.shape[1] // 2
    if not base:
        high, low = parts_of(x_ref[...])
        x_parts[:, :cases] = high
        x_parts[:, cases:] = low
    count = m_parts.shape[0] // 2 if with_modes else 0
    pair_ref, *cross_refs = outs
    index = place_ref[base // 2]
    half = rows_ref.shape[1] // 2
    chunks = half // cases
    lanes = lax.broadcasted_iota(jnp.int32, (half, order), 1)
    tall = half + chunks * count
    for k, face in enumerate((cross_face(base, index), pair_face(base, index))):
        for b in range(2):
            target, at = pair_ref, b * tall
            if k == 0:
                target, at = (cross_refs[0], at) if len(cross_refs) == 1 else (cross_refs[b], 0)
            column = column_of(rows_ref[pl.ds(face, 1), b * half : (b + 1) * half])
            picked = jnp.where(column == lanes, 1.0, 0.0).astype(BF16)
            got = dot(picked, x_parts[...])
            target[at : at + half] = got[:, :cases] + got[:, cases:]
            if with_modes:
                got = dot_nt(m_parts[...], picked)
                got = got[:count] + got[count:]
                for c in range(chunks):
                    begin = at + half + c * count
                    target[begin : begin + count] = got[:, c * cases : (c + 1) * cases]


def to_faces(base, place, rows, x, modes=None):
    order, cases = x.shape[0], x.shape[1] // (2 if base else 1)
    half = rows.shape[1] // 2
    tall = half
    args, scratch = [place, rows, x], []
    if modes is not None:
        count = modes.shape[0] // (2 if base else 1)
        tall += half // cases * count
        args = [place, rows, x, modes] if base else [place, rows, in_hbm(x), in_hbm(modes)]
        if not base:
            scratch = [pltpu.VMEM(arg.shape, arg.dtype) for arg in (x, modes)]
            scratch.append(pltpu.SemaphoreType.DMA((2,)))
    whole, part = shaped((2 * tall, cases)), shaped((tall, cases))
    outs = [whole, whole]
    if not base:
        outs = [whole, part, part, shaped((order, 2 * cases), BF16)]
        if modes is not None:
            outs.append(shaped((2 * count, order), BF16))
    return call(
        functools.partial(face_kernel, base, modes is not None),
        ("row" if base == 0 else "col") + "_faces",
        args,
        [SMEM, VMEM] + [HBM if scratch else VMEM] * (len(args) - 2),
        outs,
        scratch,
        8,
        2 * order * order * cases,
    )


def faces_of(kinds, place_ref):
    return [(cross_face if cross else pair_face)(base, place_ref[base // 2]) for base, cross in kinds]


def take_blocks(faces, adj_ref, blocks, half, count, r_parts):
    cases = blocks[0][0].shape[1]
    chunks = half // cases
    tall = half + chunks * count
    if count:
        r_parts[:, 2 * cases :] = jnp.zeros((r_parts.shape[0], r_parts.shape[1] - 2 * cases), BF16)
    for k, (face, block) in enumerate(zip(faces, blocks)):
        glued = adj_ref[face].astype(F32)
        for b in range(2):
            source, at = (block[b], 0) if len(block) == 2 else (block[0], b * tall)
            high, low = parts_of(source[at : at + half] * glued)
            begin = (2 * k + b) * half
            r_parts[begin : begin + half, :cases] = high
            r_parts[begin : begin + half, cases : 2 * cases] = low
            for c in range(chunks if count else 0):
                modes = at + half + c * count
                both = parts_of(jnp.transpose(source[modes : modes + count] * glued))
                rows = slice(begin + c * cases, begin + (c + 1) * cases)
                lane = 2 * cases + 2 * k * count
                r_parts[rows, lane : lane + 2 * count] = jnp.concatenate(both, axis=1)


def placed_rows(faces, rows_ref, begin, tile):
    ids = lax.broadcasted_iota(jnp.int32, (tile, rows_ref.shape[1]), 0) + begin
    return [jnp.where(rows_ref[pl.ds(face, 1), :] == ids, 1.0, 0.0) for face in faces]


def add_kernel(kinds, shape, last, tile, place_ref, adj_ref, rows_ref, x_ref, *refs):
    if last:
        modes_ref, sums_ref, *refs = refs
        *refs, out_ref, coef_ref, r_parts = refs
    else:
        *refs, out_ref, r_parts = refs
    order, cases = x_ref.shape
    faces = faces_of(kinds, place_ref)
    blocks = [[refs.pop(0) for _ in range(n)] for n in shape]
    take_blocks(faces, adj_ref, blocks, rows_ref.shape[1] // 2, 0, r_parts)

    @pl.loop(0, order // tile)
    def _(i):
        rows = tile_rows(i, tile)
        ones = placed_rows(faces, rows_ref, i * tile, tile)
        placed = jnp.concatenate([one.astype(BF16) for one in ones], axis=1)
        total = dot(placed, r_parts[...])
        out_ref[rows] = x_ref[rows] + (total[:, :cases] + total[:, cases:])

    if last:
        count = modes_ref.shape[0]
        coef_ref[:count] = dot3(parts_of(modes_ref[...]), parts_of(out_ref[...]))
        coef_ref[count:] = sums_ref[...]


def add_faces(kinds, place, adj, rows, x, blocks, ahead=None, tile=512):
    order, cases = x.shape
    args = [place, adj, rows, x] + list(ahead or []) + in_vmem(x for block in blocks for x in block)
    outs = [shaped((order, cases))]
    if ahead:
        outs.append(shaped((ahead[0].shape[0] + PAD, cases)))
    return call(
        functools.partial(add_kernel, kinds, [len(b) for b in blocks], bool(ahead), tile),
        "last_add" if ahead else "add",
        args,
        [SMEM, SMEM] + [VMEM] * (len(args) - 2),
        outs,
        [pltpu.VMEM((len(kinds) * rows.shape[1], 2 * cases), BF16)],
        6,
        len(kinds) * order * order * cases,
    )


def start_kernel(kinds, shape, last, count, tile, place_ref, adj_ref, rows_ref, x_ref, *refs):
    if last:
        glued_ref, near_ref, contact_ref, modes_ref, *refs = refs
        *refs, s_ref, w_high, w_low, weight_ref, clamp_ref, coef_ref, r_parts = refs
    else:
        op_ref, *refs = refs
        *refs, s_ref, near_ref, glued_ref, held, r_parts, sem = refs
        copy = pltpu.make_async_copy(op_ref, held, sem)
        copy.start()
    order, cases = x_ref.shape
    faces = faces_of(kinds, place_ref)
    blocks = [[refs.pop(0) for _ in range(n)] for n in shape]
    take_blocks(faces, adj_ref, blocks, rows_ref.shape[1] // 2, count, r_parts)

    @pl.loop(0, order // tile)
    def _(i):
        rows = tile_rows(i, tile)
        ones = placed_rows(faces, rows_ref, i * tile, tile)
        glued = jnp.zeros((tile, 1), F32)
        for face, one in zip(faces, ones):
            glued += adj_ref[face].astype(F32) * jnp.sum(one, axis=1, keepdims=True)
        total = dot(jnp.concatenate([one.astype(BF16) for one in ones], axis=1), r_parts[...])
        s = x_ref[rows] + (total[:, :cases] + total[:, cases : 2 * cases])
        near = []
        for k in range(len(faces)):
            lane = 2 * cases + 2 * k * count
            near.append(total[:, lane : lane + count] + total[:, lane + count : lane + 2 * count])
        if not last:
            s_ref[rows] = s
            near_ref[rows] = jnp.concatenate(near, axis=1)
            glued_ref[rows] = glued
        else:
            s_ref[rows] = -s
            row_free = 1.0 - (glued + glued_ref[rows])
            weight_ref[rows] = 0.5 + 0.5 * row_free
            contact = column_of(contact_ref[:, rows].astype(F32))
            clamp_ref[rows] = jnp.where(contact * row_free > 0.5, 1.0, 0.0)
            own = jnp.transpose(modes_ref[:, rows])
            high, low = parts_of(jnp.concatenate([own, near_ref[rows]] + near, axis=1))
            w_high[rows] = high
            w_low[rows] = low

    if last:
        coef_ref[...] = dot3(parts_of(modes_ref[...]), parts_of(s_ref[...]))
    else:
        copy.wait()


def start(kinds, place, adj, rows, x, blocks, count, op=None, ahead=None, tile=512):
    order, cases = x.shape
    column = shaped((order, 1))
    args = [place, adj, rows, x] + list(ahead or [in_hbm(op)]) + in_vmem(x for block in blocks for x in block)
    specs = [SMEM, SMEM, VMEM, VMEM] + [VMEM if ahead else HBM] + [VMEM] * (len(args) - 5)
    scratch = [pltpu.VMEM((len(kinds) * rows.shape[1], 2 * cases + 2 * len(kinds) * count), BF16)]
    if ahead:
        w = shaped((order, 5 * count), BF16)
        outs = [shaped((order, cases)), w, w, column, column, shaped((count, cases))]
    else:
        outs = [shaped((order, cases)), shaped((order, len(kinds) * count)), column, shaped(op.shape, op.dtype)]
        scratch.append(pltpu.SemaphoreType.DMA(()))
    return call(
        functools.partial(start_kernel, kinds, [len(b) for b in blocks], bool(ahead), count, tile),
        "last_start" if ahead else "start",
        args,
        specs,
        outs,
        scratch,
        10,
        len(kinds) * order * order * cases,
    )


def coarse_kernel(offsets, extra, grid_rows, place_ref, *refs):
    inverse_refs, refs = refs[:grid_rows], refs[grid_rows:]
    pieces = refs[: len(offsets)]
    outs = refs[len(offsets) : len(offsets) + grid_rows]
    coef, amounts = refs[len(offsets) + grid_rows :]
    row, col = place_ref[0], place_ref[1]
    count = inverse_refs[0].shape[1] // 3
    tall = count + extra
    sums = None
    for piece, inside in zip(pieces, offsets):
        for k, offset in enumerate(inside):
            begin = pl.multiple_of((col ^ offset) * count, count)
            coef[pl.ds(begin, count)] = piece[k * tall : k * tall + count]
            if extra:
                term = piece[k * tall + count : (k + 1) * tall]
                sums = term if sums is None else sums + term
    tiles = inverse_refs[0].shape[0]
    inverse = [jnp.concatenate([ref[k] for k in range(tiles)], axis=1) for ref in inverse_refs]
    inverse = parts_of(jnp.concatenate(inverse, axis=0))
    amounts[...] = dot3(inverse, parts_of(coef[...])).reshape(amounts.shape)
    odd = col % 2
    for j in range(grid_rows):
        target = row ^ j
        cross = jnp.clip(target - 1 + 2 * (target % 2), 0, grid_rows - 1) ^ row
        order = (j * 3 + 1, j * 3 + 2 - 2 * odd, j * 3 + 2 * odd, (j ^ 1) * 3 + 1, cross * 3 + 1)
        for k, source in enumerate(order):
            outs[j][k * count : (k + 1) * count] = amounts[source]
        if extra:
            outs[j][5 * count :] = sums


def coarse(place, inverse, pieces, offsets, extra):
    grid_rows = len(inverse)
    tiles, three, width = inverse[0].shape
    count = three // 3
    cases = pieces[0].shape[1]
    args = [place, *in_vmem(inverse), *in_vmem(pieces)]
    return call(
        functools.partial(coarse_kernel, offsets, extra, grid_rows),
        "coarse",
        args,
        [SMEM] + [VMEM] * (len(args) - 1),
        [shaped((5 * count + extra, cases))] * grid_rows,
        [pltpu.VMEM((tiles * width, cases), F32), pltpu.VMEM((grid_rows * 3, count, cases), F32)],
        4,
        6 * grid_rows * three * tiles * width * cases,
    )


def first_kernel(tile, op_ref, s_ref, w_high, w_low, clamp_ref, *refs):
    *part_refs, d_ref, v_ref, field = refs
    order, cases = s_ref.shape
    amount = parts_of(total_of(part_refs))

    @pl.loop(0, order // tile)
    def _(i):
        rows = tile_rows(i, tile)
        d = s_ref[rows] - dot3((w_high[rows], w_low[rows]), amount)
        d_ref[rows] = d
        h = jnp.where(clamp_ref[rows] > 0.5, jnp.maximum(-d, 0.0), -d)
        high, low = parts_of(h)
        field[rows, :cases] = high
        field[rows, cases:] = low

    @pl.loop(0, order // tile)
    def _(i):
        rows = tile_rows(i, tile)
        got = dot(op_ref[rows], field[...])
        v_ref[rows] = got[:, :cases] + got[:, cases:]


def first(op, s, w, clamp, amounts, tile=512):
    order, cases = s.shape
    args = [op, s, *w, clamp, *in_vmem(amounts)]
    return call(
        functools.partial(first_kernel, tile),
        "first",
        args,
        [VMEM] * len(args),
        [shaped((order, cases))] * 2,
        [pltpu.VMEM((order, 2 * cases), BF16)],
        6,
        4 * order * order * cases,
    )


def add_sums(sums_ref, tile, op_ref, d_ref, weight_ref, field):
    sums_ref[...] = jnp.zeros_like(sums_ref)

    @pl.loop(0, d_ref.shape[0] // tile)
    def _(i):
        rows = tile_rows(i, tile)
        operated = dot(op_ref[rows], field[...])
        d = d_ref[rows]
        sums_ref[0:1] += jnp.sum(weight_ref[rows] * d * d, axis=0, keepdims=True)
        sums_ref[1:2] += jnp.sum(d * operated, axis=0, keepdims=True)


def sums_kernel(tile, op_ref, d_ref, weight_ref, sums_ref, field):
    field[...] = d_ref[...].astype(BF16)
    add_sums(sums_ref, tile, op_ref, d_ref, weight_ref, field)


def step_sums(op, d, weight, tile=512):
    order, cases = d.shape
    return call(
        functools.partial(sums_kernel, tile),
        "step_sums",
        [op, d, weight],
        [VMEM] * 3,
        [shaped((PAD, cases))],
        [pltpu.VMEM((order, cases), BF16)],
        4,
        2 * order * order * cases,
    )[0]


def second_kernel(tile, op_ref, s_ref, d0_ref, w_high, w_low, weight_ref, *refs):
    *part_refs, d_ref, sums_ref, step_ref, field = refs
    order, cases = s_ref.shape
    wide = w_high.shape[1]
    amount = total_of(part_refs)
    length = amount[wide : wide + 1] / amount[wide + 1 : wide + 2]
    step_ref[...] = jnp.broadcast_to(length, step_ref.shape)
    amount = parts_of(amount[:wide])

    @pl.loop(0, order // tile)
    def _(i):
        rows = tile_rows(i, tile)
        q = s_ref[rows] - dot3((w_high[rows], w_low[rows]), amount)
        d = length * q + d0_ref[rows]
        d_ref[rows] = d
        field[rows] = d.astype(BF16)

    add_sums(sums_ref, tile, op_ref, d_ref, weight_ref, field)


def second(op, s, d0, w, weight, amounts, tile=512):
    order, cases = s.shape
    args = [op, s, d0, *w, weight, *in_vmem(amounts)]
    return call(
        functools.partial(second_kernel, tile),
        "second",
        args,
        [VMEM] * len(args),
        [shaped((order, cases)), shaped((PAD, cases)), shaped((PAD, cases))],
        [pltpu.VMEM((order, cases), BF16)],
        4,
        2 * order * order * cases,
    )


def finish_kernel(d0_ref, d1_ref, clamp_ref, step_ref, *refs):
    *sum_refs, out_ref = refs
    sums = total_of(sum_refs)
    low = jnp.where(clamp_ref[...] > 0.5, 0.0, -jnp.inf)
    once = jnp.maximum(-(step_ref[0:1] * d0_ref[...]), low)
    length = sums[0:1] / sums[1:2]
    out_ref[...] = jnp.maximum(once - length * d1_ref[...], low)


def finish(d0, d1, clamp, step, sums, tile=512):
    order, cases = d0.shape
    block = pl.BlockSpec((tile, cases), lambda i: (i, 0))
    small = pl.BlockSpec((PAD, cases), lambda i: (0, 0))
    return pl.pallas_call(
        finish_kernel,
        grid=(order // tile,),
        in_specs=[block, block, pl.BlockSpec((tile, 1), lambda i: (i, 0))] + [small] * (1 + len(sums)),
        out_specs=block,
        out_shape=jax.ShapeDtypeStruct((order, cases), F32),
        compiler_params=pltpu.CompilerParams(vmem_limit_bytes=16 * MIB),
        cost_estimate=pl.CostEstimate(flops=4 * order * cases, bytes_accessed=12 * order * cases, transcendentals=0),
        name="finish",
    )(d0, d1, clamp, step, *sums)


def send(x, axis, target):
    size = lax.axis_size(axis)
    pairs = [(i, target(i)) for i in range(size)]
    return lax.ppermute(x, axis, [(i, j) for i, j in pairs if j is not None and 0 <= j < size])


def swap(x, axis, bits):
    return send(x, axis, lambda i: i ^ bits)


def other_side(i):
    return i + 1 if i % 2 else i - 1


def row_exchange(pair, first_half, second_half):
    size = lax.axis_size("row")
    inside = lambda i: 0 <= other_side(i) < size
    one = send(first_half, "row", lambda i: i ^ 1 if inside(i) else None)
    two = send(second_half, "row", lambda i: (i + 2 if i % 2 else i - 2) if inside(i) else None)
    got = swap(pair, "row", 1)
    last = lambda: (
        send(one, "row", lambda i: (i - 2 if i % 2 else i + 2)),
        send(two, "row", lambda i: i ^ 1 if (0 <= (i - 2 if i % 2 else i + 2) < size) else None),
    )
    return got, (one, two), last


def col_exchange(pair, cross):
    return swap(pair, "col", 1), send(cross, "col", other_side)


def gather_cols(block):
    size = lax.axis_size("col")
    far = list(range(2, size, 2))
    pieces = [block] + [swap(block, "col", j) for j in far]
    held = jnp.concatenate(pieces, axis=0)
    known = [0] + far
    return pieces + [swap(held, "col", 1)], [[j] for j in known] + [[j ^ 1 for j in known]]


def coarse_amounts(place, inverse, block, extra):
    pieces, offsets = gather_cols(block)
    sends = coarse(place, inverse, pieces, offsets, extra)
    return [sends[0]] + [swap(sends[j], "row", j) for j in range(1, lax.axis_size("row"))]


def spread_cols(tile_block, count):
    grid_cols, tile_cols = lax.axis_size("col"), tile_block.shape[1]
    blocks = tile_block.reshape(grid_cols, count, tile_cols)
    three = jnp.concatenate([jnp.roll(blocks, 1, 0), blocks, jnp.roll(blocks, -1, 0)], axis=1)
    return three


def by_row(three):
    grid_rows = lax.axis_size("row")
    tiles = three.shape[0] // grid_rows
    row = lax.axis_index("row")
    return [lax.dynamic_slice_in_dim(three, (row ^ j) * tiles, tiles, 0) for j in range(grid_rows)]


def spread_rows(picked):
    return [picked[0]] + [swap(picked[j], "row", j) for j in range(1, len(picked))]


def after(x, *others):
    return lax.optimization_barrier((x, *others))[0]


EARLY = ((2, False), (2, True), (0, False))
LATE = ((0, True),)


def per_device(local_ops, loads, modes, coarse_inverse, face_rows, adjacency, contact):
    op, load, mode = local_ops[0, 0], loads[0, 0], modes[0, 0]
    rows, adj = face_rows[0, 0], adjacency[0, 0]
    touch = contact[0, 0][None]
    count = mode.shape[0]
    place = jnp.stack([lax.axis_index("row"), lax.axis_index("col")]).astype(jnp.int32)

    *row_sends, x_parts, m_parts = to_faces(0, place, rows, load, mode)
    pair, way, forward = row_exchange(*row_sends)
    three = spread_cols(after(coarse_inverse, row_sends[0]), count)
    col_sends = to_faces(2, after(place, three, *way), rows, x_parts, m_parts)
    three = lax.all_to_all(three, "col", 0, 0, tiled=True)
    col_got = col_exchange(*col_sends)
    blocks = [[col_got[0]], [col_got[1]], [pair]]
    part, near, glued, op = start(EARLY, place, adj, rows, load, blocks, count, op)
    picked = by_row(three)
    inverse = spread_rows(picked)
    s0, w_high, w_low, weight, clamp, coef = start(
        LATE, after(place, *picked), adj, rows, part, [forward()], count, None, [glued, near, touch, mode]
    )
    w = (w_high, w_low)
    amounts = coarse_amounts(place, inverse, coef, 0)
    d0, v = first(op, s0, w, clamp, amounts)

    *row_sends, x_parts = to_faces(0, place, rows, v)
    pair, way, forward = row_exchange(*row_sends)
    sums = step_sums(op, d0, after(weight, row_sends[0]))
    col_sends = to_faces(2, after(place, sums, *way), rows, x_parts)
    col_got = col_exchange(*col_sends)
    blocks = [[col_got[0]], [col_got[1]], [pair]]
    (part,) = add_faces(EARLY, place, adj, rows, v, blocks)
    s1, coef = add_faces(LATE, place, adj, rows, part, [forward()], [mode, sums])
    amounts = coarse_amounts(place, inverse, coef, PAD)
    d1, sums, step = second(op, s1, d0, w, weight, amounts)

    grid_rows, grid_cols = lax.axis_size("row"), lax.axis_size("col")
    sums = sum((swap(sums, "row", j) for j in range(1, grid_rows)), sums)
    sums = sum((swap(sums, "col", j) for j in range(2, grid_cols, 2)), sums)
    return finish(d0, d1, clamp, step, [sums, swap(sums, "col", 1)])[None, None]


def solution(mesh):
    placed = (
        P("row", "col", None, None),
        P("row", "col", None, None),
        P("row", "col", None, None),
        P("row", "col"),
        P("row", "col", None, None),
        P("row", "col", None),
        P("row", "col", None),
    )
    return jax.shard_map(
        per_device,
        mesh=mesh,
        in_specs=placed,
        out_specs=P("row", "col", None, None),
        check_vma=False,
    )
```

```python
import functools

import jax
import jax.numpy as jnp
from jax import lax
from jax.experimental import pallas as pl
from jax.experimental.pallas import tpu as pltpu
from jax.sharding import PartitionSpec as P

F32 = jnp.float32
BF16 = jnp.bfloat16
PAD = 8
GRANT = 8 * 1024 * 1024
LIGHT = ("step_sums", "add")
VMEM = pl.BlockSpec(memory_space=pltpu.VMEM)
SMEM = pl.BlockSpec(memory_space=pltpu.SMEM)
HBM = pl.BlockSpec(memory_space=pltpu.HBM)


def dot(a, b):
    return lax.dot_general(a, b, (((1,), (0,)), ((), ())), preferred_element_type=F32)


def dot_nt(a, b):
    return lax.dot_general(a, b, (((1,), (1,)), ((), ())), preferred_element_type=F32)


def parts_of(x):
    high = x.astype(BF16)
    return high, (x - high.astype(F32)).astype(BF16)


def dot3(a, b):
    return dot(a[0], b[0]) + (dot(a[0], b[1]) + dot(a[1], b[0]))


def column_of(row, lanes=128):
    return jnp.transpose(jnp.broadcast_to(row, (lanes, row.shape[1])))[:, :1]


def total_of(refs):
    value = refs[0][...]
    for ref in refs[1:]:
        value = value + ref[...]
    return value


def call(kernel, name, args, in_specs, outs, scratch, flops, aliases=None):
    moved = sum(x.size * x.dtype.itemsize for x in args)
    if name in LIGHT:
        flops, moved = flops // 100, moved // 100
    return pl.pallas_call(
        kernel,
        in_specs=in_specs,
        out_specs=[VMEM] * len(outs),
        out_shape=outs,
        scratch_shapes=scratch,
        compiler_params=pltpu.CompilerParams(vmem_limit_bytes=GRANT),
        cost_estimate=pl.CostEstimate(flops=int(flops), bytes_accessed=int(moved), transcendentals=0),
        input_output_aliases=aliases or {},
        name=name,
    )(*args)


def in_hbm(x):
    return pltpu.with_memory_space_constraint(x, pltpu.HBM)


def in_vmem(arrays):
    return [pltpu.with_memory_space_constraint(x, pltpu.VMEM) for x in arrays]


def shaped(shape, dtype=F32):
    return pltpu.VMEM(shape, dtype)


def pair_face(base, index):
    return base + 1 - index % 2


def cross_face(base, index):
    return base + index % 2


def splits(grid_rows):
    return grid_rows if grid_rows == 4 else 0


def has_cross(index, size):
    return jnp.logical_and(index > 0, index < size - 1)


def face_kernel(base, with_modes, split, place_ref, *refs):
    if base:
        rows_ref, x_parts, *refs = refs
        if with_modes:
            m_parts, *refs = refs
        outs = refs
    elif with_modes:
        sources, refs = refs[:4], refs[4:]
        *outs, x_parts, m_parts, rows_ref, three_ref, x_ref, modes_ref, tile_ref, sems = refs
        copies = [
            pltpu.make_async_copy(source, held, sems.at[k])
            for k, (source, held) in enumerate(zip(sources, (rows_ref, x_ref, modes_ref, tile_ref)))
        ]
        for copy in copies:
            copy.start()
        for copy in copies:
            copy.wait()
        high, low = parts_of(modes_ref[...])
        count = modes_ref.shape[0]
        m_parts[:count] = high
        m_parts[count:] = low
        size = three_ref.shape[0]
        for c in range(size):
            for k in range(3):
                begin = (c + k - 1) % size * count
                three_ref[c, k * count : (k + 1) * count] = tile_ref[begin : begin + count]
    else:
        rows_ref, x_ref, *outs, x_parts = refs
    order, cases = x_parts.shape[0], x_parts.shape[1] // 2
    if not base:
        high, low = parts_of(x_ref[...])
        x_parts[:, :cases] = high
        x_parts[:, cases:] = low
    count = m_parts.shape[0] // 2 if with_modes else 0
    index = place_ref[base // 2]
    half = rows_ref.shape[1] // 2
    chunks = half // cases
    lanes = lax.broadcasted_iota(jnp.int32, (half, order), 1)
    tall = half + chunks * count
    pair, cross = pair_face(base, index), cross_face(base, index)
    places = [(outs[0], 0, pair, 0), (outs[0], tall, pair, 1), (outs[1], 0, cross, 0), (outs[1], tall, cross, 1)]
    if split:
        inner = has_cross(index, split)
        both_ref, other_ref, last_ref = outs[:3]
        places = [
            (both_ref, 0, jnp.where(inner, cross, pair), 0),
            (both_ref, tall, pair, jnp.where(inner, 0, 1)),
            (other_ref, 0, cross, 1),
            (last_ref, 0, pair, 1),
        ]
    for target, at, face, b in places:
        if isinstance(b, int):
            row = rows_ref[pl.ds(face, 1), b * half : (b + 1) * half]
        else:
            row = jnp.where(b == 0, rows_ref[pl.ds(face, 1), :half], rows_ref[pl.ds(face, 1), half:])
        picked = jnp.where(column_of(row) == lanes, 1.0, 0.0).astype(BF16)
        got = dot(picked, x_parts[...])
        target[at : at + half] = got[:, :cases] + got[:, cases:]
        if with_modes:
            got = dot_nt(m_parts[...], picked)
            got = got[:count] + got[count:]
            for c in range(chunks):
                begin = at + half + c * count
                target[begin : begin + count] = got[:, c * cases : (c + 1) * cases]


def to_faces(base, place, rows, x, modes=None, tile_block=None):
    order, cases = x.shape[0], x.shape[1] // (2 if base else 1)
    half = rows.shape[1] // 2
    tall = half
    args, scratch = [place, rows, x], []
    if modes is not None:
        count = modes.shape[0] // (2 if base else 1)
        tall += half // cases * count
        args = [place, rows, x, modes]
    whole, part = shaped((2 * tall, cases)), shaped((tall, cases))
    split = 0 if base else splits(lax.axis_size("row"))
    outs = [whole, part, part] if split else [whole, whole]
    if not base:
        outs.append(shaped((order, 2 * cases), BF16))
        if modes is not None:
            args = [place] + [in_hbm(arg) for arg in (rows, x, modes, tile_block)]
            outs += [shaped((2 * count, order), BF16), shaped(rows.shape, rows.dtype)]
            outs.append(shaped((tile_block.shape[0] // count, 3 * count, tile_block.shape[1])))
            scratch = [pltpu.VMEM(arg.shape, F32) for arg in (x, modes, tile_block)]
            scratch.append(pltpu.SemaphoreType.DMA((4,)))
    return call(
        functools.partial(face_kernel, base, modes is not None, split),
        ("row" if base == 0 else "col") + "_faces",
        args,
        [SMEM] + [HBM if scratch else VMEM] * (len(args) - 1),
        outs,
        scratch,
        2 * order * order * cases,
    )


def faces_of(kinds, place_ref):
    return [(cross_face if cross else pair_face)(base, place_ref[base // 2]) for base, cross in kinds]


def halves_of(blocks, tall, index):
    if len(blocks) == 3:
        both, last, other = (block[...] for block in blocks)
        inner = has_cross(index, 4)
        second = jnp.where(inner, both[tall:], last)
        return [(jnp.where(inner, both[:tall], both[tall:]), second), (other, last)]
    return [(block[:tall], block[tall:]) for block in blocks]


def take_blocks(faces, adj_ref, blocks, index, half, count, r_parts, m_parts):
    cases = blocks[0].shape[1]
    chunks = half // cases
    tall = half + chunks * count
    if count:
        m_parts[...] = jnp.zeros_like(m_parts)
    for k, (face, halves) in enumerate(zip(faces, halves_of(blocks, tall, index))):
        glued = adj_ref[face].astype(F32)
        for b, source in enumerate(halves):
            high, low = parts_of(source[:half] * glued)
            begin = (2 * k + b) * half
            r_parts[begin : begin + half, :cases] = high
            r_parts[begin : begin + half, cases:] = low
            for c in range(chunks if count else 0):
                modes = half + c * count
                both = parts_of(jnp.transpose(source[modes : modes + count] * glued))
                rows = slice(begin + c * cases, begin + (c + 1) * cases)
                m_parts[rows, 2 * k * count : 2 * (k + 1) * count] = jnp.concatenate(both, axis=1)


def placed_rows(faces, rows_ref, begin, tile):
    ids = lax.broadcasted_iota(jnp.int32, (tile, rows_ref.shape[1]), 0) + begin
    return [jnp.where(rows_ref[pl.ds(face, 1), :] == ids, 1.0, 0.0) for face in faces]


def add_kernel(kinds, n_blocks, first, last, extra, count, tile, place_ref, adj_ref, rows_ref, x_ref, *refs):
    refs = list(refs)
    modes_ref = refs.pop(0) if last else None
    sums_ref = refs.pop(0) if extra else None
    blocks = [refs.pop(0) for _ in range(n_blocks)]
    out_ref = refs.pop(0)
    coef_ref = refs.pop(0) if last else None
    m_parts = refs.pop(0) if count else None
    r_parts = refs.pop(0)
    if first:
        copy = pltpu.make_async_copy(x_ref, out_ref, refs.pop(0))
        copy.start()
    order, cases = out_ref.shape
    faces = faces_of(kinds, place_ref)
    take_blocks(faces, adj_ref, blocks, place_ref[0], rows_ref.shape[1] // 2, count, r_parts, m_parts)
    if first:
        copy.wait()
        x_ref = out_ref
    sign = -1.0 if count and last else 1.0
    for i in range(order // tile):
        rows = slice(i * tile, (i + 1) * tile)
        ones = placed_rows(faces, rows_ref, i * tile, tile)
        total = dot(jnp.concatenate([one.astype(BF16) for one in ones], axis=1), r_parts[...])
        out_ref[rows] = sign * (x_ref[rows] + (total[:, :cases] + total[:, cases:]))
    if last:
        coef_ref[: modes_ref.shape[0]] = dot3(parts_of(modes_ref[...]), parts_of(out_ref[...]))
    if extra:
        coef_ref[modes_ref.shape[0] :] = sums_ref[...]


def add_faces(kinds, place, adj, rows, x, blocks, modes=None, sums=None, first=False, count=0, tile=256):
    order, cases = x.shape
    last, extra = modes is not None, sums is not None
    args = [place, adj, rows, in_hbm(x) if first else x] + [modes] * last + [sums] * extra
    args += in_vmem(blocks)
    specs = [VMEM] * len(args)
    specs[:2] = [SMEM, SMEM]
    specs[3] = HBM if first else VMEM
    outs = [shaped((order, cases))]
    if last:
        outs.append(shaped((modes.shape[0] + PAD * extra, cases)))
    if count:
        outs.append(shaped((len(kinds) * rows.shape[1], 2 * len(kinds) * count), BF16))
    scratch = [pltpu.VMEM((len(kinds) * rows.shape[1], 2 * cases), BF16)]
    if first:
        scratch.append(pltpu.SemaphoreType.DMA(()))
    return call(
        functools.partial(add_kernel, kinds, len(blocks), first, last, extra, count, tile),
        "last_add" if last else "add",
        args,
        specs,
        outs,
        scratch,
        len(kinds) * order * order * cases,
        None if first else {3: 0},
    )


def extend_kernel(groups, tile, place_ref, adj_ref, rows_ref, contact_ref, op_ref, modes_source, *refs):
    parts, refs = refs[: len(groups)], refs[len(groups) :]
    w_high, w_low, weight_ref, clamp_ref, held, modes_ref, sems = refs
    copy = pltpu.make_async_copy(op_ref, held, sems.at[0])
    modes_copy = pltpu.make_async_copy(modes_source, modes_ref, sems.at[1])
    modes_copy.start()
    copy.start()
    modes_copy.wait()
    count = modes_ref.shape[0]
    for i in range(held.shape[0] // tile):
        rows = slice(i * tile, (i + 1) * tile)
        glued = jnp.zeros((tile, 1), F32)
        blocks = [jnp.transpose(modes_ref[:, rows])]
        for kinds, part in zip(groups, parts):
            faces = faces_of(kinds, place_ref)
            ones = placed_rows(faces, rows_ref, i * tile, tile)
            for face, one in zip(faces, ones):
                glued += adj_ref[face].astype(F32) * jnp.sum(one, axis=1, keepdims=True)
            near = dot(jnp.concatenate([one.astype(BF16) for one in ones], axis=1), part[...])
            for k in range(len(faces)):
                lane = 2 * k * count
                blocks.append(near[:, lane : lane + count] + near[:, lane + count : lane + 2 * count])
        row_free = 1.0 - glued
        weight_ref[rows] = 0.5 + 0.5 * row_free
        contact = column_of(contact_ref[:, rows].astype(F32))
        clamp_ref[rows] = jnp.where(contact * row_free > 0.5, 1.0, 0.0)
        high, low = parts_of(jnp.concatenate(blocks, axis=1))
        w_high[rows] = high
        w_low[rows] = low
    copy.wait()


def extend(groups, place, adj, rows, contact, op, modes, parts, tile=256):
    order, count = op.shape[0], modes.shape[0]
    args = [place, adj, rows, contact, in_hbm(op), in_hbm(modes), *parts]
    w, column = shaped((order, 5 * count), BF16), shaped((order, 1))
    return call(
        functools.partial(extend_kernel, groups, tile),
        "extend",
        args,
        [SMEM, SMEM, VMEM, VMEM, HBM, HBM] + [VMEM] * len(parts),
        [w, w, column, column, shaped(op.shape, op.dtype)],
        [pltpu.VMEM(modes.shape, modes.dtype), pltpu.SemaphoreType.DMA((2,))],
        2 * order * order * 8 * count,
    )


def coarse_kernel(offsets, extra, grid_rows, place_ref, *refs):
    inverse_refs, refs = refs[:grid_rows], refs[grid_rows:]
    pieces = refs[: len(offsets)]
    outs = refs[len(offsets) : len(offsets) + grid_rows]
    coef, amounts = refs[len(offsets) + grid_rows :]
    row, col = place_ref[0], place_ref[1]
    count = inverse_refs[0].shape[1] // 3
    tall = count + extra
    sums = None
    for piece, inside in zip(pieces, offsets):
        for k, offset in enumerate(inside):
            begin = pl.multiple_of((col ^ offset) * count, count)
            coef[pl.ds(begin, count)] = piece[k * tall : k * tall + count]
            if extra:
                term = piece[k * tall + count : (k + 1) * tall]
                sums = term if sums is None else sums + term
    tiles = inverse_refs[0].shape[0]
    inverse = [jnp.concatenate([ref[k] for k in range(tiles)], axis=1) for ref in inverse_refs]
    inverse = parts_of(jnp.concatenate(inverse, axis=0))
    amounts[...] = dot3(inverse, parts_of(coef[...])).reshape(amounts.shape)
    odd = col % 2
    for j in range(grid_rows):
        target = row ^ j
        cross = jnp.clip(target - 1 + 2 * (target % 2), 0, grid_rows - 1) ^ row
        order = (j * 3 + 1, j * 3 + 2 - 2 * odd, j * 3 + 2 * odd, (j ^ 1) * 3 + 1, cross * 3 + 1)
        for k, source in enumerate(order):
            outs[j][k * count : (k + 1) * count] = amounts[source]
        if extra:
            outs[j][5 * count :] = sums


def coarse(place, inverse, pieces, offsets, extra):
    grid_rows = len(inverse)
    tiles, three, width = inverse[0].shape
    count = three // 3
    cases = pieces[0].shape[1]
    args = [place, *in_vmem(inverse), *in_vmem(pieces)]
    return call(
        functools.partial(coarse_kernel, offsets, extra, grid_rows),
        "coarse",
        args,
        [SMEM] + [VMEM] * (len(args) - 1),
        [shaped((5 * count + extra, cases))] * grid_rows,
        [pltpu.VMEM((tiles * width, cases), F32), pltpu.VMEM((grid_rows * 3, count, cases), F32)],
        6 * grid_rows * three * tiles * width * cases,
    )


def first_kernel(tile, op_ref, s_ref, w_high, w_low, clamp_ref, *refs):
    *part_refs, d_ref, v_ref, field = refs
    order, cases = s_ref.shape
    amount = parts_of(total_of(part_refs))

    for i in range(order // tile):
        rows = slice(i * tile, (i + 1) * tile)
        d = s_ref[rows] - dot3((w_high[rows], w_low[rows]), amount)
        d_ref[rows] = d
        h = jnp.where(clamp_ref[rows] > 0.5, jnp.maximum(-d, 0.0), -d)
        high, low = parts_of(h)
        field[rows, :cases] = high
        field[rows, cases:] = low

    for i in range(order // tile):
        rows = slice(i * tile, (i + 1) * tile)
        got = dot(op_ref[rows], field[...])
        v_ref[rows] = got[:, :cases] + got[:, cases:]


def first(op, s, w, clamp, amounts, tile=512):
    order, cases = s.shape
    args = [op, s, *w, clamp, *in_vmem(amounts)]
    return call(
        functools.partial(first_kernel, tile),
        "first",
        args,
        [VMEM] * len(args),
        [shaped((order, cases))] * 2,
        [pltpu.VMEM((order, 2 * cases), BF16)],
        4 * order * order * cases,
        {1: 0},
    )


def add_sums(sums_ref, tile, op_ref, d_ref, weight_ref, field):
    sums_ref[...] = jnp.zeros_like(sums_ref)

    for i in range(d_ref.shape[0] // tile):
        rows = slice(i * tile, (i + 1) * tile)
        operated = dot(op_ref[rows], field[...])
        d = d_ref[rows]
        sums_ref[0:1] += jnp.sum(weight_ref[rows] * d * d, axis=0, keepdims=True)
        sums_ref[1:2] += jnp.sum(d * operated, axis=0, keepdims=True)


def sums_kernel(tile, op_ref, d_ref, weight_ref, sums_ref, field):
    field[...] = d_ref[...].astype(BF16)
    add_sums(sums_ref, tile, op_ref, d_ref, weight_ref, field)


def step_sums(op, d, weight, tile=512):
    order, cases = d.shape
    return call(
        functools.partial(sums_kernel, tile),
        "step_sums",
        [op, d, weight],
        [VMEM] * 3,
        [shaped((PAD, cases))],
        [pltpu.VMEM((order, cases), BF16)],
        2 * order * order * cases,
    )[0]


def second_kernel(tile, op_ref, s_ref, d0_ref, w_high, w_low, weight_ref, *refs):
    *part_refs, d_ref, sums_ref, step_ref, field = refs
    order, cases = s_ref.shape
    wide = w_high.shape[1]
    amount = total_of(part_refs)
    length = amount[wide : wide + 1] / amount[wide + 1 : wide + 2]
    step_ref[...] = jnp.broadcast_to(length, step_ref.shape)
    amount = parts_of(amount[:wide])

    for i in range(order // tile):
        rows = slice(i * tile, (i + 1) * tile)
        q = s_ref[rows] - dot3((w_high[rows], w_low[rows]), amount)
        d = length * q + d0_ref[rows]
        d_ref[rows] = d
        field[rows] = d.astype(BF16)

    add_sums(sums_ref, tile, op_ref, d_ref, weight_ref, field)


def second(op, s, d0, w, weight, amounts, tile=512):
    order, cases = s.shape
    args = [op, s, d0, *w, weight, *in_vmem(amounts)]
    return call(
        functools.partial(second_kernel, tile),
        "second",
        args,
        [VMEM] * len(args),
        [shaped((order, cases)), shaped((PAD, cases)), shaped((PAD, cases))],
        [pltpu.VMEM((order, cases), BF16)],
        2 * order * order * cases,
        {1: 0},
    )


def finish_kernel(d0_ref, d1_ref, clamp_ref, step_ref, *refs):
    *sum_refs, out_ref = refs
    sums = total_of(sum_refs)
    low = jnp.where(clamp_ref[...] > 0.5, 0.0, -jnp.inf)
    once = jnp.maximum(-(step_ref[0:1] * d0_ref[...]), low)
    length = sums[0:1] / sums[1:2]
    out_ref[...] = jnp.maximum(once - length * d1_ref[...], low)


def finish(d0, d1, clamp, step, sums, tile=512):
    order, cases = d0.shape
    block = pl.BlockSpec((tile, cases), lambda i: (i, 0))
    small = pl.BlockSpec((PAD, cases), lambda i: (0, 0))
    return pl.pallas_call(
        finish_kernel,
        grid=(order // tile,),
        in_specs=[block, block, pl.BlockSpec((tile, 1), lambda i: (i, 0))] + [small] * (1 + len(sums)),
        out_specs=block,
        out_shape=jax.ShapeDtypeStruct((order, cases), F32),
        compiler_params=pltpu.CompilerParams(vmem_limit_bytes=GRANT),
        cost_estimate=pl.CostEstimate(flops=4 * order * cases, bytes_accessed=12 * order * cases, transcendentals=0),
        name="finish",
    )(d0, d1, clamp, step, *sums)


def send(x, axis, target):
    size = lax.axis_size(axis)
    pairs = [(i, target(i)) for i in range(size)]
    return lax.ppermute(x, axis, [(i, j) for i, j in pairs if j is not None and 0 <= j < size])


def swap(x, axis, bits):
    return send(x, axis, lambda i: i ^ bits)


def other_side(i):
    return i + 1 if i % 2 else i - 1


def row_exchange(*sends):
    size = lax.axis_size("row")
    if not splits(size):
        got = [swap(sends[0], "row", 1), send(sends[1], "row", other_side)]
        return got, got
    both, other, last = sends
    tall = other.shape[0]
    both = swap(both, "row", 1)
    other = send(other, "row", lambda i: i ^ 2 if i in (1, 2) else None)
    inner = has_cross(lax.axis_index("row"), size)
    got_last = swap(jnp.where(inner, last, other), "row", 1)
    got_other = send(both[:tall], "row", lambda i: i ^ 2 if i in (0, 3) else None)
    return [both, other], [both, got_last, got_other]


def col_exchange(pair, cross):
    return swap(pair, "col", 1), send(cross, "col", other_side)


def gather_cols(block):
    size = lax.axis_size("col")
    far = list(range(2, size, 2))
    pieces = [block] + [swap(block, "col", j) for j in far]
    held = jnp.concatenate(pieces, axis=0)
    known = [0] + far
    return pieces + [swap(held, "col", 1)], [[j] for j in known] + [[j ^ 1 for j in known]]


def coarse_amounts(place, inverse, block, extra):
    pieces, offsets = gather_cols(block)
    sends = coarse(place, inverse, pieces, offsets, extra)
    return [sends[0]] + [swap(sends[j], "row", j) for j in range(1, lax.axis_size("row"))], sends[0]


def by_row(three):
    grid_rows = lax.axis_size("row")
    tiles = three.shape[0] // grid_rows
    row = lax.axis_index("row")
    return [lax.dynamic_slice_in_dim(three, (row ^ j) * tiles, tiles, 0) for j in range(grid_rows)]


def spread_rows(picked):
    return [picked[0]] + [swap(picked[j], "row", j) for j in range(1, len(picked))]


def after(x, *others):
    return lax.optimization_barrier((x, *others))[0]


def after_all(arrays, others):
    return lax.optimization_barrier((*arrays, *others))[: len(arrays)]


COLS = ((2, False), (2, True))
ROWS = ((0, False), (0, True))


def per_device(local_ops, loads, modes, coarse_inverse, face_rows, adjacency, contact):
    op, load, mode = local_ops[0, 0], loads[0, 0], modes[0, 0]
    rows, adj = face_rows[0, 0], adjacency[0, 0]
    touch = contact[0, 0][None]
    count = mode.shape[0]
    place = jnp.stack([lax.axis_index("row"), lax.axis_index("col")]).astype(jnp.int32)

    *row_sends, x_parts, m_parts, rows, three = to_faces(0, place, rows, load, mode, coarse_inverse)
    way, row_got = row_exchange(*row_sends)
    col_sends = to_faces(2, place, rows, x_parts, m_parts)
    col_got = col_exchange(*after_all(col_sends, way))
    picked = by_row(lax.all_to_all(after(three, *col_sends), "col", 0, 0, tiled=True))
    inverse = spread_rows(picked)
    part, m_cols = add_faces(COLS, place, adj, rows, load, col_got, first=True, count=count)
    s0, coef, m_rows = add_faces(ROWS, after(place, *picked), adj, rows, part, row_got, modes=mode, count=count)
    amounts, own = coarse_amounts(place, inverse, after(coef, *inverse), 0)
    w_high, w_low, weight, clamp, op = extend(
        (COLS, ROWS), after(place, own), adj, rows, touch, op, mode, (m_cols, m_rows)
    )
    w = (w_high, w_low)
    d0, v = first(op, s0, w, clamp, amounts)

    *row_sends, x_parts = to_faces(0, place, rows, v)
    way, row_got = row_exchange(*row_sends)
    col_sends = to_faces(2, place, rows, x_parts)
    sums = step_sums(op, d0, after(weight, *col_sends))
    col_got = col_exchange(*after_all(col_sends, [*way[1:], sums]))
    (part,) = add_faces(COLS, place, adj, rows, v, col_got)
    s1, coef = add_faces(ROWS, place, adj, rows, part, row_got, mode, sums)
    amounts, _ = coarse_amounts(place, inverse, coef, PAD)
    d1, sums, step = second(op, s1, d0, w, weight, amounts)

    grid_rows, grid_cols = lax.axis_size("row"), lax.axis_size("col")
    sums = sum((swap(sums, "row", j) for j in range(1, grid_rows)), sums)
    sums = sum((swap(sums, "col", j) for j in range(2, grid_cols, 2)), sums)
    return finish(d0, d1, clamp, step, [sums, swap(sums, "col", 1)])[None, None]


def solution(mesh):
    placed = (
        P("row", "col", None, None),
        P("row", "col", None, None),
        P("row", "col", None, None),
        P("row", "col"),
        P("row", "col", None, None),
        P("row", "col", None),
        P("row", "col", None),
    )
    return jax.shard_map(
        per_device,
        mesh=mesh,
        in_specs=placed,
        out_specs=P("row", "col", None, None),
        check_vma=False,
    )
```

```python
import functools

import jax
import jax.numpy as jnp
from jax import lax
from jax.experimental import pallas as pl
from jax.experimental.pallas import tpu as pltpu
from jax.sharding import PartitionSpec as P

F32 = jnp.float32
BF16 = jnp.bfloat16
PAD = 8
GRANT = 8 * 1024 * 1024
UNROLL = dict(add=1, extend=1, prepare=1, first=2, sums=2)
LIGHT = ("step_sums", "add")
VMEM = pl.BlockSpec(memory_space=pltpu.VMEM)
SMEM = pl.BlockSpec(memory_space=pltpu.SMEM)
HBM = pl.BlockSpec(memory_space=pltpu.HBM)


def dot(a, b):
    return lax.dot_general(a, b, (((1,), (0,)), ((), ())), preferred_element_type=F32)


def dot_nt(a, b):
    return lax.dot_general(a, b, (((1,), (1,)), ((), ())), preferred_element_type=F32)


def parts_of(x):
    high = x.astype(BF16)
    return high, (x - high.astype(F32)).astype(BF16)


def dot3(a, b):
    return dot(a[0], b[0]) + (dot(a[0], b[1]) + dot(a[1], b[0]))


def column_of(row, lanes=128):
    return jnp.transpose(jnp.broadcast_to(row, (lanes, row.shape[1])))[:, :1]


def over_tiles(order, tile, unroll, body):
    @pl.loop(0, order // tile, unroll=unroll)
    def _(i):
        begin = pl.multiple_of(i * tile, tile)
        body(begin, pl.ds(begin, tile))


def total_of(refs):
    value = refs[0][...]
    for ref in refs[1:]:
        value = value + ref[...]
    return value


def call(kernel, name, args, in_specs, outs, scratch, flops, aliases=None):
    moved = sum(x.size * x.dtype.itemsize for x in args)
    if name in LIGHT:
        flops, moved = flops // 100, moved // 100
    return pl.pallas_call(
        kernel,
        in_specs=in_specs,
        out_specs=[VMEM] * len(outs),
        out_shape=outs,
        scratch_shapes=scratch,
        compiler_params=pltpu.CompilerParams(vmem_limit_bytes=GRANT),
        cost_estimate=pl.CostEstimate(flops=int(flops), bytes_accessed=int(moved), transcendentals=0),
        input_output_aliases=aliases or {},
        name=name,
    )(*args)


def in_hbm(x):
    return pltpu.with_memory_space_constraint(x, pltpu.HBM)


def in_vmem(arrays):
    return [pltpu.with_memory_space_constraint(x, pltpu.VMEM) for x in arrays]


def shaped(shape, dtype=F32):
    return pltpu.VMEM(shape, dtype)


def pair_face(base, index):
    return base + 1 - index % 2


def cross_face(base, index):
    return base + index % 2


def splits(grid_rows):
    return grid_rows if grid_rows == 4 else 0


def has_cross(index, size):
    return jnp.logical_and(index > 0, index < size - 1)


def face_kernel(base, with_modes, split, place_ref, *refs):
    if base:
        rows_ref, x_parts, *refs = refs
        if with_modes:
            m_parts, *refs = refs
        outs = refs
    elif with_modes:
        sources, refs = refs[:4], refs[4:]
        *outs, x_parts, m_parts, rows_ref, three_ref, x_ref, modes_ref, tile_ref, sems = refs
        copies = [
            pltpu.make_async_copy(source, held, sems.at[k])
            for k, (source, held) in enumerate(zip(sources, (rows_ref, x_ref, modes_ref, tile_ref)))
        ]
        for copy in copies:
            copy.start()
        for copy in copies:
            copy.wait()
        high, low = parts_of(modes_ref[...])
        count = modes_ref.shape[0]
        m_parts[:count] = high
        m_parts[count:] = low
        size = three_ref.shape[0]
        for c in range(size):
            for k in range(3):
                begin = (c + k - 1) % size * count
                three_ref[c, k * count : (k + 1) * count] = tile_ref[begin : begin + count]
    else:
        rows_ref, x_ref, *outs, x_parts = refs
    order, cases = x_parts.shape[0], x_parts.shape[1] // 2
    if not base:
        high, low = parts_of(x_ref[...])
        x_parts[:, :cases] = high
        x_parts[:, cases:] = low
    count = m_parts.shape[0] // 2 if with_modes else 0
    index = place_ref[base // 2]
    half = rows_ref.shape[1] // 2
    chunks = half // cases
    lanes = lax.broadcasted_iota(jnp.int32, (half, order), 1)
    tall = half + chunks * count
    pair, cross = pair_face(base, index), cross_face(base, index)
    places = [(outs[0], 0, pair, 0), (outs[0], tall, pair, 1), (outs[1], 0, cross, 0), (outs[1], tall, cross, 1)]
    if split:
        inner = has_cross(index, split)
        both_ref, other_ref, last_ref = outs[:3]
        places = [
            (both_ref, 0, jnp.where(inner, cross, pair), 0),
            (both_ref, tall, pair, jnp.where(inner, 0, 1)),
            (other_ref, 0, cross, 1),
            (last_ref, 0, pair, 1),
        ]
    for target, at, face, b in places:
        if isinstance(b, int):
            row = rows_ref[pl.ds(face, 1), b * half : (b + 1) * half]
        else:
            row = jnp.where(b == 0, rows_ref[pl.ds(face, 1), :half], rows_ref[pl.ds(face, 1), half:])
        picked = jnp.where(column_of(row) == lanes, 1.0, 0.0).astype(BF16)
        got = dot(picked, x_parts[...])
        target[at : at + half] = got[:, :cases] + got[:, cases:]
        if with_modes:
            got = dot_nt(m_parts[...], picked)
            got = got[:count] + got[count:]
            for c in range(chunks):
                begin = at + half + c * count
                target[begin : begin + count] = got[:, c * cases : (c + 1) * cases]


def to_faces(base, place, rows, x, modes=None, tile_block=None):
    order, cases = x.shape[0], x.shape[1] // (2 if base else 1)
    half = rows.shape[1] // 2
    tall = half
    args, scratch = [place, rows, x], []
    if modes is not None:
        count = modes.shape[0] // (2 if base else 1)
        tall += half // cases * count
        args = [place, rows, x, modes]
    whole, part = shaped((2 * tall, cases)), shaped((tall, cases))
    split = 0 if base else splits(lax.axis_size("row"))
    outs = [whole, part, part] if split else [whole, whole]
    if not base:
        outs.append(shaped((order, 2 * cases), BF16))
        if modes is not None:
            args = [place] + [in_hbm(arg) for arg in (rows, x, modes, tile_block)]
            outs += [shaped((2 * count, order), BF16), shaped(rows.shape, rows.dtype)]
            outs.append(shaped((tile_block.shape[0] // count, 3 * count, tile_block.shape[1])))
            scratch = [pltpu.VMEM(arg.shape, F32) for arg in (x, modes, tile_block)]
            scratch.append(pltpu.SemaphoreType.DMA((4,)))
    return call(
        functools.partial(face_kernel, base, modes is not None, split),
        ("row" if base == 0 else "col") + "_faces",
        args,
        [SMEM] + [HBM if scratch else VMEM] * (len(args) - 1),
        outs,
        scratch,
        2 * order * order * cases,
    )


def faces_of(kinds, place_ref):
    return [(cross_face if cross else pair_face)(base, place_ref[base // 2]) for base, cross in kinds]


def halves_of(blocks, tall, index):
    if len(blocks) == 3:
        both, last, other = (block[...] for block in blocks)
        inner = has_cross(index, 4)
        second = jnp.where(inner, both[tall:], last)
        return [(jnp.where(inner, both[:tall], both[tall:]), second), (other, last)]
    return [(block[:tall], block[tall:]) for block in blocks]


def take_blocks(faces, adj_ref, blocks, index, half, count, r_parts, m_parts):
    cases = blocks[0].shape[1]
    chunks = half // cases
    tall = half + chunks * count
    if count:
        m_parts[...] = jnp.zeros_like(m_parts)
    for k, (face, halves) in enumerate(zip(faces, halves_of(blocks, tall, index))):
        glued = adj_ref[face].astype(F32)
        for b, source in enumerate(halves):
            high, low = parts_of(source[:half] * glued)
            begin = (2 * k + b) * half
            r_parts[begin : begin + half, :cases] = high
            r_parts[begin : begin + half, cases:] = low
            for c in range(chunks if count else 0):
                modes = half + c * count
                both = parts_of(jnp.transpose(source[modes : modes + count] * glued))
                rows = slice(begin + c * cases, begin + (c + 1) * cases)
                m_parts[rows, 2 * k * count : 2 * (k + 1) * count] = jnp.concatenate(both, axis=1)


def placed_rows(faces, rows_ref, begin, tile):
    ids = lax.broadcasted_iota(jnp.int32, (tile, rows_ref.shape[1]), 0) + begin
    return [jnp.where(rows_ref[pl.ds(face, 1), :] == ids, 1.0, 0.0) for face in faces]


def add_kernel(kinds, n_blocks, first, last, extra, count, tile, place_ref, adj_ref, rows_ref, x_ref, *refs):
    refs = list(refs)
    modes_ref = refs.pop(0) if last else None
    sums_ref = refs.pop(0) if extra else None
    blocks = [refs.pop(0) for _ in range(n_blocks)]
    out_ref = refs.pop(0)
    coef_ref = refs.pop(0) if last else None
    m_parts = refs.pop(0) if count else None
    r_parts = refs.pop(0)
    if first:
        copy = pltpu.make_async_copy(x_ref, out_ref, refs.pop(0))
        copy.start()
    order, cases = out_ref.shape
    faces = faces_of(kinds, place_ref)
    take_blocks(faces, adj_ref, blocks, place_ref[0], rows_ref.shape[1] // 2, count, r_parts, m_parts)
    if first:
        copy.wait()
        x_ref = out_ref
    sign = -1.0 if count and last else 1.0

    def body(begin, rows):
        ones = placed_rows(faces, rows_ref, begin, tile)
        total = dot(jnp.concatenate([one.astype(BF16) for one in ones], axis=1), r_parts[...])
        out_ref[rows] = sign * (x_ref[rows] + (total[:, :cases] + total[:, cases:]))

    over_tiles(order, tile, UNROLL["add"], body)
    if last:
        coef_ref[: modes_ref.shape[0]] = dot3(parts_of(modes_ref[...]), parts_of(out_ref[...]))
    if extra:
        coef_ref[modes_ref.shape[0] :] = sums_ref[...]


def add_faces(kinds, place, adj, rows, x, blocks, modes=None, sums=None, first=False, count=0, tile=512):
    order, cases = x.shape
    last, extra = modes is not None, sums is not None
    args = [place, adj, rows, in_hbm(x) if first else x] + [modes] * last + [sums] * extra
    args += in_vmem(blocks)
    specs = [VMEM] * len(args)
    specs[:2] = [SMEM, SMEM]
    specs[3] = HBM if first else VMEM
    outs = [shaped((order, cases))]
    if last:
        outs.append(shaped((modes.shape[0] + PAD * extra, cases)))
    if count:
        outs.append(shaped((len(kinds) * rows.shape[1], 2 * len(kinds) * count), BF16))
    scratch = [pltpu.VMEM((len(kinds) * rows.shape[1], 2 * cases), BF16)]
    if first:
        scratch.append(pltpu.SemaphoreType.DMA(()))
    return call(
        functools.partial(add_kernel, kinds, len(blocks), first, last, extra, count, tile),
        "last_add" if last else "add",
        args,
        specs,
        outs,
        scratch,
        len(kinds) * order * order * cases,
        None if first else {3: 0},
    )


def extend_kernel(groups, tile, place_ref, adj_ref, rows_ref, contact_ref, op_ref, modes_source, *refs):
    parts, refs = refs[: len(groups)], refs[len(groups) :]
    w_high, w_low, weight_ref, clamp_ref, held, modes_ref, sems = refs
    copy = pltpu.make_async_copy(op_ref, held, sems.at[0])
    modes_copy = pltpu.make_async_copy(modes_source, modes_ref, sems.at[1])
    modes_copy.start()
    copy.start()
    modes_copy.wait()
    count = modes_ref.shape[0]

    def body(begin, rows):
        glued = jnp.zeros((tile, 1), F32)
        blocks = [jnp.transpose(modes_ref[:, rows])]
        for kinds, part in zip(groups, parts):
            faces = faces_of(kinds, place_ref)
            ones = placed_rows(faces, rows_ref, begin, tile)
            for face, one in zip(faces, ones):
                glued += adj_ref[face].astype(F32) * jnp.sum(one, axis=1, keepdims=True)
            near = dot(jnp.concatenate([one.astype(BF16) for one in ones], axis=1), part[...])
            for k in range(len(faces)):
                lane = 2 * k * count
                blocks.append(near[:, lane : lane + count] + near[:, lane + count : lane + 2 * count])
        row_free = 1.0 - glued
        weight_ref[rows] = 0.5 + 0.5 * row_free
        contact = column_of(contact_ref[:, rows].astype(F32))
        clamp_ref[rows] = jnp.where(contact * row_free > 0.5, 1.0, 0.0)
        high, low = parts_of(jnp.concatenate(blocks, axis=1))
        w_high[rows] = high
        w_low[rows] = low

    over_tiles(held.shape[0], tile, UNROLL["extend"], body)
    copy.wait()


def extend(groups, place, adj, rows, contact, op, modes, parts, tile=256):
    order, count = op.shape[0], modes.shape[0]
    args = [place, adj, rows, contact, in_hbm(op), in_hbm(modes), *parts]
    w, column = shaped((order, 5 * count), BF16), shaped((order, 1))
    return call(
        functools.partial(extend_kernel, groups, tile),
        "extend",
        args,
        [SMEM, SMEM, VMEM, VMEM, HBM, HBM] + [VMEM] * len(parts),
        [w, w, column, column, shaped(op.shape, op.dtype)],
        [pltpu.VMEM(modes.shape, modes.dtype), pltpu.SemaphoreType.DMA((2,))],
        2 * order * order * 8 * count,
    )


def coarse_kernel(offsets, extra, grid_rows, place_ref, *refs):
    inverse_refs, refs = refs[:grid_rows], refs[grid_rows:]
    pieces = refs[: len(offsets)]
    outs = refs[len(offsets) : len(offsets) + grid_rows]
    coef, amounts = refs[len(offsets) + grid_rows :]
    row, col = place_ref[0], place_ref[1]
    count = inverse_refs[0].shape[1] // 3
    tall = count + extra
    sums = None
    for piece, inside in zip(pieces, offsets):
        for k, offset in enumerate(inside):
            begin = pl.multiple_of((col ^ offset) * count, count)
            coef[pl.ds(begin, count)] = piece[k * tall : k * tall + count]
            if extra:
                term = piece[k * tall + count : (k + 1) * tall]
                sums = term if sums is None else sums + term
    tiles = inverse_refs[0].shape[0]
    inverse = [jnp.concatenate([ref[k] for k in range(tiles)], axis=1) for ref in inverse_refs]
    inverse = parts_of(jnp.concatenate(inverse, axis=0))
    amounts[...] = dot3(inverse, parts_of(coef[...])).reshape(amounts.shape)
    odd = col % 2
    for j in range(grid_rows):
        target = row ^ j
        cross = jnp.clip(target - 1 + 2 * (target % 2), 0, grid_rows - 1) ^ row
        order = (j * 3 + 1, j * 3 + 2 - 2 * odd, j * 3 + 2 * odd, (j ^ 1) * 3 + 1, cross * 3 + 1)
        for k, source in enumerate(order):
            outs[j][k * count : (k + 1) * count] = amounts[source]
        if extra:
            outs[j][5 * count :] = sums


def coarse(place, inverse, pieces, offsets, extra):
    grid_rows = len(inverse)
    tiles, three, width = inverse[0].shape
    count = three // 3
    cases = pieces[0].shape[1]
    args = [place, *in_vmem(inverse), *in_vmem(pieces)]
    return call(
        functools.partial(coarse_kernel, offsets, extra, grid_rows),
        "coarse",
        args,
        [SMEM] + [VMEM] * (len(args) - 1),
        [shaped((5 * count + extra, cases))] * grid_rows,
        [pltpu.VMEM((tiles * width, cases), F32), pltpu.VMEM((grid_rows * 3, count, cases), F32)],
        6 * grid_rows * three * tiles * width * cases,
    )


def first_kernel(tile, op_ref, s_ref, w_high, w_low, clamp_ref, *refs):
    *part_refs, d_ref, v_ref, field = refs
    order, cases = s_ref.shape
    amount = parts_of(total_of(part_refs))


    def prepare(_, rows):
        d = s_ref[rows] - dot3((w_high[rows], w_low[rows]), amount)
        d_ref[rows] = d
        h = jnp.where(clamp_ref[rows] > 0.5, jnp.maximum(-d, 0.0), -d)
        high, low = parts_of(h)
        field[rows, :cases] = high
        field[rows, cases:] = low

    def body(_, rows):
        got = dot(op_ref[rows], field[...])
        v_ref[rows] = got[:, :cases] + got[:, cases:]

    over_tiles(order, tile, UNROLL["prepare"], prepare)
    over_tiles(order, tile, UNROLL["first"], body)


def first(op, s, w, clamp, amounts, tile=512):
    order, cases = s.shape
    args = [op, s, *w, clamp, *in_vmem(amounts)]
    return call(
        functools.partial(first_kernel, tile),
        "first",
        args,
        [VMEM] * len(args),
        [shaped((order, cases))] * 2,
        [pltpu.VMEM((order, 2 * cases), BF16)],
        4 * order * order * cases,
        {1: 0},
    )


def add_sums(sums_ref, tile, op_ref, d_ref, weight_ref, field):
    sums_ref[...] = jnp.zeros_like(sums_ref)


    def body(_, rows):
        operated = dot(op_ref[rows], field[...])
        d = d_ref[rows]
        sums_ref[0:1] += jnp.sum(weight_ref[rows] * d * d, axis=0, keepdims=True)
        sums_ref[1:2] += jnp.sum(d * operated, axis=0, keepdims=True)

    over_tiles(d_ref.shape[0], tile, UNROLL["sums"], body)


def sums_kernel(tile, op_ref, d_ref, weight_ref, sums_ref, field):
    field[...] = d_ref[...].astype(BF16)
    add_sums(sums_ref, tile, op_ref, d_ref, weight_ref, field)


def step_sums(op, d, weight, tile=512):
    order, cases = d.shape
    return call(
        functools.partial(sums_kernel, tile),
        "step_sums",
        [op, d, weight],
        [VMEM] * 3,
        [shaped((PAD, cases))],
        [pltpu.VMEM((order, cases), BF16)],
        2 * order * order * cases,
    )[0]


def second_kernel(tile, op_ref, s_ref, d0_ref, w_high, w_low, weight_ref, *refs):
    *part_refs, d_ref, sums_ref, step_ref, field = refs
    order, cases = s_ref.shape
    wide = w_high.shape[1]
    amount = total_of(part_refs)
    length = amount[wide : wide + 1] / amount[wide + 1 : wide + 2]
    step_ref[...] = jnp.broadcast_to(length, step_ref.shape)
    amount = parts_of(amount[:wide])


    def prepare(_, rows):
        q = s_ref[rows] - dot3((w_high[rows], w_low[rows]), amount)
        d = length * q + d0_ref[rows]
        d_ref[rows] = d
        field[rows] = d.astype(BF16)

    over_tiles(order, tile, UNROLL["prepare"], prepare)
    add_sums(sums_ref, tile, op_ref, d_ref, weight_ref, field)


def second(op, s, d0, w, weight, amounts, tile=512):
    order, cases = s.shape
    args = [op, s, d0, *w, weight, *in_vmem(amounts)]
    return call(
        functools.partial(second_kernel, tile),
        "second",
        args,
        [VMEM] * len(args),
        [shaped((order, cases)), shaped((PAD, cases)), shaped((PAD, cases))],
        [pltpu.VMEM((order, cases), BF16)],
        2 * order * order * cases,
        {1: 0},
    )


def finish_kernel(d0_ref, d1_ref, clamp_ref, step_ref, *refs):
    *sum_refs, out_ref = refs
    sums = total_of(sum_refs)
    low = jnp.where(clamp_ref[...] > 0.5, 0.0, -jnp.inf)
    once = jnp.maximum(-(step_ref[0:1] * d0_ref[...]), low)
    length = sums[0:1] / sums[1:2]
    out_ref[...] = jnp.maximum(once - length * d1_ref[...], low)


def finish(d0, d1, clamp, step, sums, tile=512):
    order, cases = d0.shape
    block = pl.BlockSpec((tile, cases), lambda i: (i, 0))
    small = pl.BlockSpec((PAD, cases), lambda i: (0, 0))
    return pl.pallas_call(
        finish_kernel,
        grid=(order // tile,),
        in_specs=[block, block, pl.BlockSpec((tile, 1), lambda i: (i, 0))] + [small] * (1 + len(sums)),
        out_specs=block,
        out_shape=jax.ShapeDtypeStruct((order, cases), F32),
        compiler_params=pltpu.CompilerParams(vmem_limit_bytes=GRANT),
        cost_estimate=pl.CostEstimate(flops=4 * order * cases, bytes_accessed=12 * order * cases, transcendentals=0),
        name="finish",
    )(d0, d1, clamp, step, *sums)


def send(x, axis, target):
    size = lax.axis_size(axis)
    pairs = [(i, target(i)) for i in range(size)]
    return lax.ppermute(x, axis, [(i, j) for i, j in pairs if j is not None and 0 <= j < size])


def swap(x, axis, bits):
    return send(x, axis, lambda i: i ^ bits)


def other_side(i):
    return i + 1 if i % 2 else i - 1


def row_exchange(*sends):
    size = lax.axis_size("row")
    if not splits(size):
        got = [swap(sends[0], "row", 1), send(sends[1], "row", other_side)]
        return got, got
    both, other, last = sends
    tall = other.shape[0]
    both = swap(both, "row", 1)
    other = send(other, "row", lambda i: i ^ 2 if i in (1, 2) else None)
    inner = has_cross(lax.axis_index("row"), size)
    got_last = swap(jnp.where(inner, last, other), "row", 1)
    got_other = send(both[:tall], "row", lambda i: i ^ 2 if i in (0, 3) else None)
    return [both, other], [both, got_last, got_other]


def col_exchange(pair, cross):
    return swap(pair, "col", 1), send(cross, "col", other_side)


def gather_cols(block):
    size = lax.axis_size("col")
    far = list(range(2, size, 2))
    pieces = [block] + [swap(block, "col", j) for j in far]
    held = jnp.concatenate(pieces, axis=0)
    known = [0] + far
    return pieces + [swap(held, "col", 1)], [[j] for j in known] + [[j ^ 1 for j in known]]


def coarse_amounts(place, inverse, block, extra):
    pieces, offsets = gather_cols(block)
    sends = coarse(place, inverse, pieces, offsets, extra)
    return [sends[0]] + [swap(sends[j], "row", j) for j in range(1, lax.axis_size("row"))], sends[0]


def by_row(three):
    grid_rows = lax.axis_size("row")
    tiles = three.shape[0] // grid_rows
    row = lax.axis_index("row")
    return [lax.dynamic_slice_in_dim(three, (row ^ j) * tiles, tiles, 0) for j in range(grid_rows)]


def spread_rows(picked):
    return [picked[0]] + [swap(picked[j], "row", j) for j in range(1, len(picked))]


def after(x, *others):
    return lax.optimization_barrier((x, *others))[0]


def after_all(arrays, others):
    return lax.optimization_barrier((*arrays, *others))[: len(arrays)]


COLS = ((2, False), (2, True))
ROWS = ((0, False), (0, True))


def per_device(local_ops, loads, modes, coarse_inverse, face_rows, adjacency, contact):
    op, load, mode = local_ops[0, 0], loads[0, 0], modes[0, 0]
    rows, adj = face_rows[0, 0], adjacency[0, 0]
    touch = contact[0, 0][None]
    count = mode.shape[0]
    place = jnp.stack([lax.axis_index("row"), lax.axis_index("col")]).astype(jnp.int32)

    *row_sends, x_parts, m_parts, rows, three = to_faces(0, place, rows, load, mode, coarse_inverse)
    way, row_got = row_exchange(*row_sends)
    col_sends = to_faces(2, place, rows, x_parts, m_parts)
    col_got = col_exchange(*after_all(col_sends, way))
    picked = by_row(lax.all_to_all(after(three, *col_sends), "col", 0, 0, tiled=True))
    inverse = spread_rows(picked)
    part, m_cols = add_faces(COLS, place, adj, rows, load, col_got, first=True, count=count)
    s0, coef, m_rows = add_faces(ROWS, after(place, *picked), adj, rows, part, row_got, modes=mode, count=count)
    amounts, own = coarse_amounts(place, inverse, after(coef, *inverse), 0)
    w_high, w_low, weight, clamp, op = extend(
        (COLS, ROWS), after(place, own), adj, rows, touch, op, mode, (m_cols, m_rows)
    )
    w = (w_high, w_low)
    d0, v = first(op, s0, w, clamp, amounts)

    *row_sends, x_parts = to_faces(0, place, rows, v)
    way, row_got = row_exchange(*row_sends)
    col_sends = to_faces(2, place, rows, x_parts)
    sums = step_sums(op, d0, after(weight, *col_sends))
    col_got = col_exchange(*after_all(col_sends, [*way[1:], sums]))
    (part,) = add_faces(COLS, place, adj, rows, v, col_got)
    s1, coef = add_faces(ROWS, place, adj, rows, part, row_got, mode, sums)
    amounts, _ = coarse_amounts(place, inverse, coef, PAD)
    d1, sums, step = second(op, s1, d0, w, weight, amounts)

    grid_rows, grid_cols = lax.axis_size("row"), lax.axis_size("col")
    sums = sum((swap(sums, "row", j) for j in range(1, grid_rows)), sums)
    sums = sum((swap(sums, "col", j) for j in range(2, grid_cols, 2)), sums)
    return finish(d0, d1, clamp, step, [sums, swap(sums, "col", 1)])[None, None]


def solution(mesh):
    placed = (
        P("row", "col", None, None),
        P("row", "col", None, None),
        P("row", "col", None, None),
        P("row", "col"),
        P("row", "col", None, None),
        P("row", "col", None),
        P("row", "col", None),
    )
    return jax.shard_map(
        per_device,
        mesh=mesh,
        in_specs=placed,
        out_specs=P("row", "col", None, None),
        check_vma=False,
    )
```

```python
import functools

import jax
import jax.numpy as jnp
from jax import lax
from jax.experimental import pallas as pl
from jax.experimental.pallas import tpu as pltpu
from jax.sharding import PartitionSpec as P

F32 = jnp.float32
BF16 = jnp.bfloat16
PAD = 8
GRANT = 8 * 1024 * 1024
UNROLL = dict(add=1, extend=1, prepare=1, first=4, sums=2)
LIGHT = ("step_sums", "add")
VMEM = pl.BlockSpec(memory_space=pltpu.VMEM)
SMEM = pl.BlockSpec(memory_space=pltpu.SMEM)
HBM = pl.BlockSpec(memory_space=pltpu.HBM)


def dot(a, b):
    return lax.dot_general(a, b, (((1,), (0,)), ((), ())), preferred_element_type=F32)


def dot_nt(a, b):
    return lax.dot_general(a, b, (((1,), (1,)), ((), ())), preferred_element_type=F32)


def parts_of(x):
    high = x.astype(BF16)
    return high, (x - high.astype(F32)).astype(BF16)


def dot3(a, b):
    return dot(a[0], b[0]) + (dot(a[0], b[1]) + dot(a[1], b[0]))


def column_of(row, lanes=128):
    return jnp.transpose(jnp.broadcast_to(row, (lanes, row.shape[1])))[:, :1]


def over_tiles(order, tile, unroll, body):
    @pl.loop(0, order // tile, unroll=unroll)
    def _(i):
        begin = pl.multiple_of(i * tile, tile)
        body(begin, pl.ds(begin, tile))


def total_of(refs):
    value = refs[0][...]
    for ref in refs[1:]:
        value = value + ref[...]
    return value


def call(kernel, name, args, in_specs, outs, scratch, flops, aliases=None):
    moved = sum(x.size * x.dtype.itemsize for x in args)
    if name in LIGHT:
        flops, moved = flops // 100, moved // 100
    return pl.pallas_call(
        kernel,
        in_specs=in_specs,
        out_specs=[VMEM] * len(outs),
        out_shape=outs,
        scratch_shapes=scratch,
        compiler_params=pltpu.CompilerParams(vmem_limit_bytes=GRANT),
        cost_estimate=pl.CostEstimate(flops=int(flops), bytes_accessed=int(moved), transcendentals=0),
        input_output_aliases=aliases or {},
        name=name,
    )(*args)


def in_hbm(x):
    return pltpu.with_memory_space_constraint(x, pltpu.HBM)


def in_vmem(arrays):
    return [pltpu.with_memory_space_constraint(x, pltpu.VMEM) for x in arrays]


def shaped(shape, dtype=F32):
    return pltpu.VMEM(shape, dtype)


def pair_face(base, index):
    return base + 1 - index % 2


def cross_face(base, index):
    return base + index % 2


def splits(grid_rows):
    return grid_rows if grid_rows == 4 else 0


def has_cross(index, size):
    return jnp.logical_and(index > 0, index < size - 1)


def face_kernel(base, with_modes, split, place_ref, *refs):
    if base:
        rows_ref, x_parts, *refs = refs
        if with_modes:
            m_parts, *refs = refs
        outs = refs
    elif with_modes:
        sources, refs = refs[:4], refs[4:]
        *outs, x_parts, m_parts, rows_ref, three_ref, x_ref, modes_ref, tile_ref, sems = refs
        copies = [
            pltpu.make_async_copy(source, held, sems.at[k])
            for k, (source, held) in enumerate(zip(sources, (rows_ref, x_ref, modes_ref, tile_ref)))
        ]
        for copy in copies:
            copy.start()
        for copy in copies:
            copy.wait()
        high, low = parts_of(modes_ref[...])
        count = modes_ref.shape[0]
        m_parts[:count] = high
        m_parts[count:] = low
        size = three_ref.shape[0]
        for c in range(size):
            for k in range(3):
                begin = (c + k - 1) % size * count
                three_ref[c, k * count : (k + 1) * count] = tile_ref[begin : begin + count]
    else:
        rows_ref, x_ref, *outs, x_parts = refs
    order, cases = x_parts.shape[0], x_parts.shape[1] // 2
    if not base:
        high, low = parts_of(x_ref[...])
        x_parts[:, :cases] = high
        x_parts[:, cases:] = low
    count = m_parts.shape[0] // 2 if with_modes else 0
    index = place_ref[base // 2]
    half = rows_ref.shape[1] // 2
    chunks = half // cases
    lanes = lax.broadcasted_iota(jnp.int32, (half, order), 1)
    tall = half + chunks * count
    pair, cross = pair_face(base, index), cross_face(base, index)
    places = [(outs[0], 0, pair, 0), (outs[0], tall, pair, 1), (outs[1], 0, cross, 0), (outs[1], tall, cross, 1)]
    if split:
        inner = has_cross(index, split)
        both_ref, other_ref, last_ref = outs[:3]
        places = [
            (both_ref, 0, jnp.where(inner, cross, pair), 0),
            (both_ref, tall, pair, jnp.where(inner, 0, 1)),
            (other_ref, 0, cross, 1),
            (last_ref, 0, pair, 1),
        ]
    for target, at, face, b in places:
        if isinstance(b, int):
            row = rows_ref[pl.ds(face, 1), b * half : (b + 1) * half]
        else:
            row = jnp.where(b == 0, rows_ref[pl.ds(face, 1), :half], rows_ref[pl.ds(face, 1), half:])
        picked = jnp.where(column_of(row) == lanes, 1.0, 0.0).astype(BF16)
        got = dot(picked, x_parts[...])
        target[at : at + half] = got[:, :cases] + got[:, cases:]
        if with_modes:
            got = dot_nt(m_parts[...], picked)
            got = got[:count] + got[count:]
            for c in range(chunks):
                begin = at + half + c * count
                target[begin : begin + count] = got[:, c * cases : (c + 1) * cases]


def to_faces(base, place, rows, x, modes=None, tile_block=None):
    order, cases = x.shape[0], x.shape[1] // (2 if base else 1)
    half = rows.shape[1] // 2
    tall = half
    args, scratch = [place, rows, x], []
    if modes is not None:
        count = modes.shape[0] // (2 if base else 1)
        tall += half // cases * count
        args = [place, rows, x, modes]
    whole, part = shaped((2 * tall, cases)), shaped((tall, cases))
    split = 0 if base else splits(lax.axis_size("row"))
    outs = [whole, part, part] if split else [whole, whole]
    if not base:
        outs.append(shaped((order, 2 * cases), BF16))
        if modes is not None:
            args = [place] + [in_hbm(arg) for arg in (rows, x, modes, tile_block)]
            outs += [shaped((2 * count, order), BF16), shaped(rows.shape, rows.dtype)]
            outs.append(shaped((tile_block.shape[0] // count, 3 * count, tile_block.shape[1])))
            scratch = [pltpu.VMEM(arg.shape, F32) for arg in (x, modes, tile_block)]
            scratch.append(pltpu.SemaphoreType.DMA((4,)))
    return call(
        functools.partial(face_kernel, base, modes is not None, split),
        ("row" if base == 0 else "col") + "_faces",
        args,
        [SMEM] + [HBM if scratch else VMEM] * (len(args) - 1),
        outs,
        scratch,
        2 * order * order * cases,
    )


def relay_kernel(place_ref, both_ref, other_ref, last_ref, pair_ref, far_ref):
    tall = far_ref.shape[0]
    pair_ref[...] = jnp.where(has_cross(place_ref[0], 4), last_ref[...], other_ref[...])
    far_ref[...] = both_ref[:tall]


def relay(place, both, other, last):
    args = [place, *in_vmem([both, other, last])]
    return call(relay_kernel, "relay", args, [SMEM] + [VMEM] * 3, [shaped(last.shape)] * 2, [], last.size)


def faces_of(kinds, place_ref):
    return [(cross_face if cross else pair_face)(base, place_ref[base // 2]) for base, cross in kinds]


def halves_of(blocks, tall, index):
    if len(blocks) == 3:
        both, last, other = (block[...] for block in blocks)
        inner = has_cross(index, 4)
        second = jnp.where(inner, both[tall:], last)
        return [(jnp.where(inner, both[:tall], both[tall:]), second), (other, last)]
    return [(block[:tall], block[tall:]) for block in blocks]


def take_blocks(faces, adj_ref, blocks, index, half, count, r_parts, m_parts):
    cases = blocks[0].shape[1]
    chunks = half // cases
    tall = half + chunks * count
    if count:
        m_parts[...] = jnp.zeros_like(m_parts)
    for k, (face, halves) in enumerate(zip(faces, halves_of(blocks, tall, index))):
        glued = adj_ref[face].astype(F32)
        for b, source in enumerate(halves):
            high, low = parts_of(source[:half] * glued)
            begin = (2 * k + b) * half
            r_parts[begin : begin + half, :cases] = high
            r_parts[begin : begin + half, cases:] = low
            for c in range(chunks if count else 0):
                modes = half + c * count
                both = parts_of(jnp.transpose(source[modes : modes + count] * glued))
                rows = slice(begin + c * cases, begin + (c + 1) * cases)
                m_parts[rows, 2 * k * count : 2 * (k + 1) * count] = jnp.concatenate(both, axis=1)


def placed_rows(faces, rows_ref, begin, tile):
    ids = lax.broadcasted_iota(jnp.int32, (tile, rows_ref.shape[1]), 0) + begin
    return [jnp.where(rows_ref[pl.ds(face, 1), :] == ids, 1.0, 0.0) for face in faces]


def add_kernel(kinds, n_blocks, first, last, extra, count, tile, place_ref, adj_ref, rows_ref, x_ref, *refs):
    refs = list(refs)
    modes_ref = refs.pop(0) if last else None
    sums_ref = refs.pop(0) if extra else None
    blocks = [refs.pop(0) for _ in range(n_blocks)]
    out_ref = refs.pop(0)
    coef_ref = refs.pop(0) if last else None
    m_parts = refs.pop(0) if count else None
    r_parts = refs.pop(0)
    if first:
        copy = pltpu.make_async_copy(x_ref, out_ref, refs.pop(0))
        copy.start()
    order, cases = out_ref.shape
    faces = faces_of(kinds, place_ref)
    take_blocks(faces, adj_ref, blocks, place_ref[0], rows_ref.shape[1] // 2, count, r_parts, m_parts)
    if first:
        copy.wait()
        x_ref = out_ref
    sign = -1.0 if count and last else 1.0

    def body(begin, rows):
        ones = placed_rows(faces, rows_ref, begin, tile)
        total = dot(jnp.concatenate([one.astype(BF16) for one in ones], axis=1), r_parts[...])
        out_ref[rows] = sign * (x_ref[rows] + (total[:, :cases] + total[:, cases:]))

    over_tiles(order, tile, UNROLL["add"], body)
    if last:
        coef_ref[: modes_ref.shape[0]] = dot3(parts_of(modes_ref[...]), parts_of(out_ref[...]))
    if extra:
        coef_ref[modes_ref.shape[0] :] = sums_ref[...]


def add_faces(kinds, place, adj, rows, x, blocks, modes=None, sums=None, first=False, count=0, tile=512):
    order, cases = x.shape
    last, extra = modes is not None, sums is not None
    args = [place, adj, rows, in_hbm(x) if first else x] + [modes] * last + [sums] * extra
    args += in_vmem(blocks)
    specs = [VMEM] * len(args)
    specs[:2] = [SMEM, SMEM]
    specs[3] = HBM if first else VMEM
    outs = [shaped((order, cases))]
    if last:
        outs.append(shaped((modes.shape[0] + PAD * extra, cases)))
    if count:
        outs.append(shaped((len(kinds) * rows.shape[1], 2 * len(kinds) * count), BF16))
    scratch = [pltpu.VMEM((len(kinds) * rows.shape[1], 2 * cases), BF16)]
    if first:
        scratch.append(pltpu.SemaphoreType.DMA(()))
    return call(
        functools.partial(add_kernel, kinds, len(blocks), first, last, extra, count, tile),
        "last_add" if last else "add",
        args,
        specs,
        outs,
        scratch,
        len(kinds) * order * order * cases,
        None if first else {3: 0},
    )


def extend_kernel(groups, tile, place_ref, adj_ref, rows_ref, contact_ref, op_ref, modes_source, *refs):
    parts, refs = refs[: len(groups)], refs[len(groups) :]
    w_high, w_low, weight_ref, clamp_ref, held, modes_ref, sems = refs
    copy = pltpu.make_async_copy(op_ref, held, sems.at[0])
    modes_copy = pltpu.make_async_copy(modes_source, modes_ref, sems.at[1])
    modes_copy.start()
    copy.start()
    modes_copy.wait()
    count = modes_ref.shape[0]

    def body(begin, rows):
        glued = jnp.zeros((tile, 1), F32)
        blocks = [jnp.transpose(modes_ref[:, rows])]
        for kinds, part in zip(groups, parts):
            faces = faces_of(kinds, place_ref)
            ones = placed_rows(faces, rows_ref, begin, tile)
            for face, one in zip(faces, ones):
                glued += adj_ref[face].astype(F32) * jnp.sum(one, axis=1, keepdims=True)
            near = dot(jnp.concatenate([one.astype(BF16) for one in ones], axis=1), part[...])
            for k in range(len(faces)):
                lane = 2 * k * count
                blocks.append(near[:, lane : lane + count] + near[:, lane + count : lane + 2 * count])
        row_free = 1.0 - glued
        weight_ref[rows] = 0.5 + 0.5 * row_free
        contact = column_of(contact_ref[:, rows].astype(F32))
        clamp_ref[rows] = jnp.where(contact * row_free > 0.5, 1.0, 0.0)
        high, low = parts_of(jnp.concatenate(blocks, axis=1))
        w_high[rows] = high
        w_low[rows] = low

    over_tiles(held.shape[0], tile, UNROLL["extend"], body)
    copy.wait()


def extend(groups, place, adj, rows, contact, op, modes, parts, tile=512):
    order, count = op.shape[0], modes.shape[0]
    args = [place, adj, rows, contact, in_hbm(op), in_hbm(modes), *parts]
    w, column = shaped((order, 5 * count), BF16), shaped((order, 1))
    return call(
        functools.partial(extend_kernel, groups, tile),
        "extend",
        args,
        [SMEM, SMEM, VMEM, VMEM, HBM, HBM] + [VMEM] * len(parts),
        [w, w, column, column, shaped(op.shape, op.dtype)],
        [pltpu.VMEM(modes.shape, modes.dtype), pltpu.SemaphoreType.DMA((2,))],
        2 * order * order * 8 * count,
    )


def coarse_kernel(offsets, extra, grid_rows, place_ref, *refs):
    inverse_refs, refs = refs[:grid_rows], refs[grid_rows:]
    pieces = refs[: len(offsets)]
    outs = refs[len(offsets) : len(offsets) + grid_rows]
    coef, amounts = refs[len(offsets) + grid_rows :]
    row, col = place_ref[0], place_ref[1]
    count = inverse_refs[0].shape[1] // 3
    tall = count + extra
    sums = None
    for piece, inside in zip(pieces, offsets):
        for k, offset in enumerate(inside):
            begin = pl.multiple_of((col ^ offset) * count, count)
            coef[pl.ds(begin, count)] = piece[k * tall : k * tall + count]
            if extra:
                term = piece[k * tall + count : (k + 1) * tall]
                sums = term if sums is None else sums + term
    tiles = inverse_refs[0].shape[0]
    inverse = [jnp.concatenate([ref[k] for k in range(tiles)], axis=1) for ref in inverse_refs]
    inverse = parts_of(jnp.concatenate(inverse, axis=0))
    amounts[...] = dot3(inverse, parts_of(coef[...])).reshape(amounts.shape)
    odd = col % 2
    for j in range(grid_rows):
        target = row ^ j
        cross = jnp.clip(target - 1 + 2 * (target % 2), 0, grid_rows - 1) ^ row
        order = (j * 3 + 1, j * 3 + 2 - 2 * odd, j * 3 + 2 * odd, (j ^ 1) * 3 + 1, cross * 3 + 1)
        for k, source in enumerate(order):
            outs[j][k * count : (k + 1) * count] = amounts[source]
        if extra:
            outs[j][5 * count :] = sums


def coarse(place, inverse, pieces, offsets, extra):
    grid_rows = len(inverse)
    tiles, three, width = inverse[0].shape
    count = three // 3
    cases = pieces[0].shape[1]
    args = [place, *in_vmem(inverse), *in_vmem(pieces)]
    return call(
        functools.partial(coarse_kernel, offsets, extra, grid_rows),
        "coarse",
        args,
        [SMEM] + [VMEM] * (len(args) - 1),
        [shaped((5 * count + extra, cases))] * grid_rows,
        [pltpu.VMEM((tiles * width, cases), F32), pltpu.VMEM((grid_rows * 3, count, cases), F32)],
        6 * grid_rows * three * tiles * width * cases,
    )


def first_kernel(tile, op_ref, s_ref, w_high, w_low, clamp_ref, *refs):
    *part_refs, d_ref, v_ref, field = refs
    order, cases = s_ref.shape
    amount = parts_of(total_of(part_refs))


    def prepare(_, rows):
        d = s_ref[rows] - dot3((w_high[rows], w_low[rows]), amount)
        d_ref[rows] = d
        h = jnp.where(clamp_ref[rows] > 0.5, jnp.maximum(-d, 0.0), -d)
        high, low = parts_of(h)
        field[rows, :cases] = high
        field[rows, cases:] = low

    def body(_, rows):
        got = dot(op_ref[rows], field[...])
        v_ref[rows] = got[:, :cases] + got[:, cases:]

    over_tiles(order, tile, UNROLL["prepare"], prepare)
    over_tiles(order, tile, UNROLL["first"], body)


def first(op, s, w, clamp, amounts, tile=512):
    order, cases = s.shape
    args = [op, s, *w, clamp, *in_vmem(amounts)]
    return call(
        functools.partial(first_kernel, tile),
        "first",
        args,
        [VMEM] * len(args),
        [shaped((order, cases))] * 2,
        [pltpu.VMEM((order, 2 * cases), BF16)],
        4 * order * order * cases,
        {1: 0},
    )


def add_sums(sums_ref, tile, op_ref, d_ref, weight_ref, field):
    sums_ref[...] = jnp.zeros_like(sums_ref)


    def body(_, rows):
        operated = dot(op_ref[rows], field[...])
        d = d_ref[rows]
        sums_ref[0:1] += jnp.sum(weight_ref[rows] * d * d, axis=0, keepdims=True)
        sums_ref[1:2] += jnp.sum(d * operated, axis=0, keepdims=True)

    over_tiles(d_ref.shape[0], tile, UNROLL["sums"], body)


def sums_kernel(tile, op_ref, d_ref, weight_ref, sums_ref, field):
    field[...] = d_ref[...].astype(BF16)
    add_sums(sums_ref, tile, op_ref, d_ref, weight_ref, field)


def step_sums(op, d, weight, tile=512):
    order, cases = d.shape
    return call(
        functools.partial(sums_kernel, tile),
        "step_sums",
        [op, d, weight],
        [VMEM] * 3,
        [shaped((PAD, cases))],
        [pltpu.VMEM((order, cases), BF16)],
        2 * order * order * cases,
    )[0]


def second_kernel(tile, op_ref, s_ref, d0_ref, w_high, w_low, weight_ref, *refs):
    *part_refs, d_ref, sums_ref, step_ref, field = refs
    order, cases = s_ref.shape
    wide = w_high.shape[1]
    amount = total_of(part_refs)
    length = amount[wide : wide + 1] / amount[wide + 1 : wide + 2]
    step_ref[...] = jnp.broadcast_to(length, step_ref.shape)
    amount = parts_of(amount[:wide])


    def prepare(_, rows):
        q = s_ref[rows] - dot3((w_high[rows], w_low[rows]), amount)
        d = length * q + d0_ref[rows]
        d_ref[rows] = d
        field[rows] = d.astype(BF16)

    over_tiles(order, tile, UNROLL["prepare"], prepare)
    add_sums(sums_ref, tile, op_ref, d_ref, weight_ref, field)


def second(op, s, d0, w, weight, amounts, tile=512):
    order, cases = s.shape
    args = [op, s, d0, *w, weight, *in_vmem(amounts)]
    return call(
        functools.partial(second_kernel, tile),
        "second",
        args,
        [VMEM] * len(args),
        [shaped((order, cases)), shaped((PAD, cases)), shaped((PAD, cases))],
        [pltpu.VMEM((order, cases), BF16)],
        2 * order * order * cases,
        {1: 0},
    )


def finish_kernel(d0_ref, d1_ref, clamp_ref, step_ref, *refs):
    *sum_refs, out_ref = refs
    sums = total_of(sum_refs)
    low = jnp.where(clamp_ref[...] > 0.5, 0.0, -jnp.inf)
    once = jnp.maximum(-(step_ref[0:1] * d0_ref[...]), low)
    length = sums[0:1] / sums[1:2]
    out_ref[...] = jnp.maximum(once - length * d1_ref[...], low)


def finish(d0, d1, clamp, step, sums, tile=512):
    order, cases = d0.shape
    block = pl.BlockSpec((tile, cases), lambda i: (i, 0))
    small = pl.BlockSpec((PAD, cases), lambda i: (0, 0))
    return pl.pallas_call(
        finish_kernel,
        grid=(order // tile,),
        in_specs=[block, block, pl.BlockSpec((tile, 1), lambda i: (i, 0))] + [small] * (1 + len(sums)),
        out_specs=block,
        out_shape=jax.ShapeDtypeStruct((order, cases), F32),
        compiler_params=pltpu.CompilerParams(vmem_limit_bytes=GRANT),
        cost_estimate=pl.CostEstimate(flops=4 * order * cases, bytes_accessed=12 * order * cases, transcendentals=0),
        name="finish",
    )(d0, d1, clamp, step, *sums)


def send(x, axis, target):
    size = lax.axis_size(axis)
    pairs = [(i, target(i)) for i in range(size)]
    return lax.ppermute(x, axis, [(i, j) for i, j in pairs if j is not None and 0 <= j < size])


def swap(x, axis, bits):
    return send(x, axis, lambda i: i ^ bits)


def other_side(i):
    return i + 1 if i % 2 else i - 1


def row_exchange(place, *sends):
    size = lax.axis_size("row")
    if not splits(size):
        got = [swap(sends[0], "row", 1), send(sends[1], "row", other_side)]
        return got, got
    both, other, last = sends
    both = swap(both, "row", 1)
    other = send(other, "row", lambda i: i ^ 2 if i in (1, 2) else None)
    to_pair, to_far = relay(place, both, other, last)
    got_last = swap(to_pair, "row", 1)
    got_other = send(to_far, "row", lambda i: i ^ 2 if i in (0, 3) else None)
    return [both, other], [both, got_last, got_other]


def col_exchange(pair, cross):
    return swap(pair, "col", 1), send(cross, "col", other_side)


def gather_cols(block):
    size = lax.axis_size("col")
    far = list(range(2, size, 2))
    pieces = [block] + [swap(block, "col", j) for j in far]
    held = jnp.concatenate(pieces, axis=0)
    known = [0] + far
    return pieces + [swap(held, "col", 1)], [[j] for j in known] + [[j ^ 1 for j in known]]


def coarse_amounts(place, inverse, block, extra):
    pieces, offsets = gather_cols(block)
    sends = coarse(place, inverse, pieces, offsets, extra)
    return [sends[0]] + [swap(sends[j], "row", j) for j in range(1, lax.axis_size("row"))], sends[0]


def by_row(three):
    grid_rows = lax.axis_size("row")
    tiles = three.shape[0] // grid_rows
    row = lax.axis_index("row")
    return [lax.dynamic_slice_in_dim(three, (row ^ j) * tiles, tiles, 0) for j in range(grid_rows)]


def spread_rows(picked):
    return [picked[0]] + [swap(picked[j], "row", j) for j in range(1, len(picked))]


def after(x, *others):
    return lax.optimization_barrier((x, *others))[0]


def after_all(arrays, others):
    return lax.optimization_barrier((*arrays, *others))[: len(arrays)]


COLS = ((2, False), (2, True))
ROWS = ((0, False), (0, True))


def per_device(local_ops, loads, modes, coarse_inverse, face_rows, adjacency, contact):
    op, load, mode = local_ops[0, 0], loads[0, 0], modes[0, 0]
    rows, adj = face_rows[0, 0], adjacency[0, 0]
    touch = contact[0, 0][None]
    count = mode.shape[0]
    place = jnp.stack([lax.axis_index("row"), lax.axis_index("col")]).astype(jnp.int32)

    *row_sends, x_parts, m_parts, rows, three = to_faces(0, place, rows, load, mode, coarse_inverse)
    way, row_got = row_exchange(place, *row_sends)
    col_sends = to_faces(2, place, rows, x_parts, m_parts)
    col_got = col_exchange(*after_all(col_sends, way))
    picked = by_row(lax.all_to_all(after(three, *col_sends), "col", 0, 0, tiled=True))
    inverse = spread_rows(picked)
    part, m_cols = add_faces(COLS, place, adj, rows, load, col_got, first=True, count=count)
    s0, coef, m_rows = add_faces(ROWS, after(place, *picked), adj, rows, part, row_got, modes=mode, count=count)
    amounts, own = coarse_amounts(place, inverse, after(coef, *inverse), 0)
    w_high, w_low, weight, clamp, op = extend(
        (COLS, ROWS), after(place, own), adj, rows, touch, op, mode, (m_cols, m_rows)
    )
    w = (w_high, w_low)
    d0, v = first(op, s0, w, clamp, amounts)

    *row_sends, x_parts = to_faces(0, place, rows, v)
    way, row_got = row_exchange(place, *row_sends)
    col_sends = to_faces(2, place, rows, x_parts)
    col_got = col_exchange(*after_all(col_sends, way[1:]))
    sums = step_sums(op, d0, after(weight, col_got[0]))
    (part,) = add_faces(COLS, place, adj, rows, v, col_got)
    s1, coef = add_faces(ROWS, place, adj, rows, part, row_got, mode, sums)
    amounts, _ = coarse_amounts(place, inverse, coef, PAD)
    d1, sums, step = second(op, s1, d0, w, weight, amounts)

    grid_rows, grid_cols = lax.axis_size("row"), lax.axis_size("col")
    sums = sum((swap(sums, "row", j) for j in range(1, grid_rows)), sums)
    sums = sum((swap(sums, "col", j) for j in range(2, grid_cols, 2)), sums)
    return finish(d0, d1, clamp, step, [sums, swap(sums, "col", 1)])[None, None]


def solution(mesh):
    placed = (
        P("row", "col", None, None),
        P("row", "col", None, None),
        P("row", "col", None, None),
        P("row", "col"),
        P("row", "col", None, None),
        P("row", "col", None),
        P("row", "col", None),
    )
    return jax.shard_map(
        per_device,
        mesh=mesh,
        in_specs=placed,
        out_specs=P("row", "col", None, None),
        check_vma=False,
    )
```

```python
import functools

import jax
import jax.numpy as jnp
from jax import lax
from jax.experimental import pallas as pl
from jax.experimental.pallas import tpu as pltpu
from jax.sharding import PartitionSpec as P

F32 = jnp.float32
BF16 = jnp.bfloat16
PAD = 8
GRANT = 8 * 1024 * 1024
UNROLL = dict(add=2, extend=1, prepare=1, first=4, sums=4)
LIGHT = ("step_sums", "add")
VMEM = pl.BlockSpec(memory_space=pltpu.VMEM)
SMEM = pl.BlockSpec(memory_space=pltpu.SMEM)
HBM = pl.BlockSpec(memory_space=pltpu.HBM)


def dot(a, b):
    return lax.dot_general(a, b, (((1,), (0,)), ((), ())), preferred_element_type=F32)


def dot_nt(a, b):
    return lax.dot_general(a, b, (((1,), (1,)), ((), ())), preferred_element_type=F32)


def parts_of(x):
    high = x.astype(BF16)
    return high, (x - high.astype(F32)).astype(BF16)


def dot3(a, b):
    return dot(a[0], b[0]) + (dot(a[0], b[1]) + dot(a[1], b[0]))


def column_of(row, lanes=128):
    return jnp.transpose(jnp.broadcast_to(row, (lanes, row.shape[1])))[:, :1]


def over_tiles(order, tile, unroll, body):
    @pl.loop(0, order // tile, unroll=unroll)
    def _(i):
        begin = pl.multiple_of(i * tile, tile)
        body(begin, pl.ds(begin, tile))


def total_of(refs):
    value = refs[0][...]
    for ref in refs[1:]:
        value = value + ref[...]
    return value


def call(kernel, name, args, in_specs, outs, scratch, flops, aliases=None):
    moved = sum(x.size * x.dtype.itemsize for x in args)
    if name in LIGHT:
        flops, moved = flops // 100, moved // 100
    return pl.pallas_call(
        kernel,
        in_specs=in_specs,
        out_specs=[VMEM] * len(outs),
        out_shape=outs,
        scratch_shapes=scratch,
        compiler_params=pltpu.CompilerParams(vmem_limit_bytes=GRANT),
        cost_estimate=pl.CostEstimate(flops=int(flops), bytes_accessed=int(moved), transcendentals=0),
        input_output_aliases=aliases or {},
        name=name,
    )(*args)


def in_hbm(x):
    return pltpu.with_memory_space_constraint(x, pltpu.HBM)


def in_vmem(arrays):
    return [pltpu.with_memory_space_constraint(x, pltpu.VMEM) for x in arrays]


def shaped(shape, dtype=F32):
    return pltpu.VMEM(shape, dtype)


def pair_face(base, index):
    return base + 1 - index % 2


def cross_face(base, index):
    return base + index % 2


def splits(grid_rows):
    return grid_rows if grid_rows == 4 else 0


def has_cross(index, size):
    return jnp.logical_and(index > 0, index < size - 1)


def face_kernel(base, with_modes, split, place_ref, *refs):
    if base:
        rows_ref, x_parts, *refs = refs
        if with_modes:
            m_parts, *refs = refs
        outs = refs
    elif with_modes:
        sources, refs = refs[:4], refs[4:]
        *outs, x_parts, m_parts, rows_ref, three_ref, x_ref, modes_ref, tile_ref, sems = refs
        copies = [
            pltpu.make_async_copy(source, held, sems.at[k])
            for k, (source, held) in enumerate(zip(sources, (rows_ref, x_ref, modes_ref, tile_ref)))
        ]
        for copy in copies:
            copy.start()
        for copy in copies:
            copy.wait()
        high, low = parts_of(modes_ref[...])
        count = modes_ref.shape[0]
        m_parts[:count] = high
        m_parts[count:] = low
        size = three_ref.shape[0]
        for c in range(size):
            for k in range(3):
                begin = (c + k - 1) % size * count
                three_ref[c, k * count : (k + 1) * count] = tile_ref[begin : begin + count]
    else:
        rows_ref, x_ref, *outs, x_parts = refs
    order, cases = x_parts.shape[0], x_parts.shape[1] // 2
    if not base:
        high, low = parts_of(x_ref[...])
        x_parts[:, :cases] = high
        x_parts[:, cases:] = low
    count = m_parts.shape[0] // 2 if with_modes else 0
    index = place_ref[base // 2]
    half = rows_ref.shape[1] // 2
    chunks = half // cases
    lanes = lax.broadcasted_iota(jnp.int32, (half, order), 1)
    tall = half + chunks * count
    pair, cross = pair_face(base, index), cross_face(base, index)
    places = [(outs[0], 0, pair, 0), (outs[0], tall, pair, 1), (outs[1], 0, cross, 0), (outs[1], tall, cross, 1)]
    if split:
        inner = has_cross(index, split)
        both_ref, other_ref, last_ref = outs[:3]
        places = [
            (both_ref, 0, jnp.where(inner, cross, pair), 0),
            (both_ref, tall, pair, jnp.where(inner, 0, 1)),
            (other_ref, 0, cross, 1),
            (last_ref, 0, pair, 1),
        ]
    for target, at, face, b in places:
        if isinstance(b, int):
            row = rows_ref[pl.ds(face, 1), b * half : (b + 1) * half]
        else:
            row = jnp.where(b == 0, rows_ref[pl.ds(face, 1), :half], rows_ref[pl.ds(face, 1), half:])
        picked = jnp.where(column_of(row) == lanes, 1.0, 0.0).astype(BF16)
        got = dot(picked, x_parts[...])
        target[at : at + half] = got[:, :cases] + got[:, cases:]
        if with_modes:
            got = dot_nt(m_parts[...], picked)
            got = got[:count] + got[count:]
            for c in range(chunks):
                begin = at + half + c * count
                target[begin : begin + count] = got[:, c * cases : (c + 1) * cases]


def to_faces(base, place, rows, x, modes=None, tile_block=None):
    order, cases = x.shape[0], x.shape[1] // (2 if base else 1)
    half = rows.shape[1] // 2
    tall = half
    args, scratch = [place, rows, x], []
    if modes is not None:
        count = modes.shape[0] // (2 if base else 1)
        tall += half // cases * count
        args = [place, rows, x, modes]
    whole, part = shaped((2 * tall, cases)), shaped((tall, cases))
    split = 0 if base else splits(lax.axis_size("row"))
    outs = [whole, part, part] if split else [whole, whole]
    if not base:
        outs.append(shaped((order, 2 * cases), BF16))
        if modes is not None:
            args = [place] + [in_hbm(arg) for arg in (rows, x, modes, tile_block)]
            outs += [shaped((2 * count, order), BF16), shaped(rows.shape, rows.dtype)]
            outs.append(shaped((tile_block.shape[0] // count, 3 * count, tile_block.shape[1])))
            scratch = [pltpu.VMEM(arg.shape, F32) for arg in (x, modes, tile_block)]
            scratch.append(pltpu.SemaphoreType.DMA((4,)))
    return call(
        functools.partial(face_kernel, base, modes is not None, split),
        ("row" if base == 0 else "col") + "_faces",
        args,
        [SMEM] + [HBM if scratch else VMEM] * (len(args) - 1),
        outs,
        scratch,
        2 * order * order * cases,
    )


def relay_kernel(place_ref, both_ref, other_ref, last_ref, pair_ref, far_ref):
    tall = far_ref.shape[0]
    pair_ref[...] = jnp.where(has_cross(place_ref[0], 4), last_ref[...], other_ref[...])
    far_ref[...] = both_ref[:tall]


def relay(place, both, other, last):
    args = [place, *in_vmem([both, other, last])]
    return call(relay_kernel, "relay", args, [SMEM] + [VMEM] * 3, [shaped(last.shape)] * 2, [], last.size)


def faces_of(kinds, place_ref):
    return [(cross_face if cross else pair_face)(base, place_ref[base // 2]) for base, cross in kinds]


def halves_of(blocks, tall, index):
    if len(blocks) == 3:
        both, last, other = (block[...] for block in blocks)
        inner = has_cross(index, 4)
        second = jnp.where(inner, both[tall:], last)
        return [(jnp.where(inner, both[:tall], both[tall:]), second), (other, last)]
    return [(block[:tall], block[tall:]) for block in blocks]


def take_blocks(faces, adj_ref, blocks, index, half, count, r_parts, m_parts):
    cases = blocks[0].shape[1]
    chunks = half // cases
    tall = half + chunks * count
    if count:
        m_parts[...] = jnp.zeros_like(m_parts)
    for k, (face, halves) in enumerate(zip(faces, halves_of(blocks, tall, index))):
        glued = adj_ref[face].astype(F32)
        for b, source in enumerate(halves):
            high, low = parts_of(source[:half] * glued)
            begin = (2 * k + b) * half
            r_parts[begin : begin + half, :cases] = high
            r_parts[begin : begin + half, cases:] = low
            for c in range(chunks if count else 0):
                modes = half + c * count
                both = parts_of(jnp.transpose(source[modes : modes + count] * glued))
                rows = slice(begin + c * cases, begin + (c + 1) * cases)
                m_parts[rows, 2 * k * count : 2 * (k + 1) * count] = jnp.concatenate(both, axis=1)


def placed_rows(faces, rows_ref, begin, tile):
    ids = lax.broadcasted_iota(jnp.int32, (tile, rows_ref.shape[1]), 0) + begin
    return [jnp.where(rows_ref[pl.ds(face, 1), :] == ids, 1.0, 0.0) for face in faces]


def add_kernel(kinds, n_blocks, first, last, extra, count, tile, place_ref, adj_ref, rows_ref, x_ref, *refs):
    refs = list(refs)
    modes_ref = refs.pop(0) if last else None
    sums_ref = refs.pop(0) if extra else None
    blocks = [refs.pop(0) for _ in range(n_blocks)]
    out_ref = refs.pop(0)
    coef_ref = refs.pop(0) if last else None
    m_parts = refs.pop(0) if count else None
    r_parts = refs.pop(0)
    if first:
        copy = pltpu.make_async_copy(x_ref, out_ref, refs.pop(0))
        copy.start()
    order, cases = out_ref.shape
    faces = faces_of(kinds, place_ref)
    take_blocks(faces, adj_ref, blocks, place_ref[0], rows_ref.shape[1] // 2, count, r_parts, m_parts)
    if first:
        copy.wait()
        x_ref = out_ref
    sign = -1.0 if count and last else 1.0

    def body(begin, rows):
        ones = placed_rows(faces, rows_ref, begin, tile)
        total = dot(jnp.concatenate([one.astype(BF16) for one in ones], axis=1), r_parts[...])
        out_ref[rows] = sign * (x_ref[rows] + (total[:, :cases] + total[:, cases:]))

    over_tiles(order, tile, UNROLL["add"], body)
    if last:
        coef_ref[: modes_ref.shape[0]] = dot3(parts_of(modes_ref[...]), parts_of(out_ref[...]))
    if extra:
        coef_ref[modes_ref.shape[0] :] = sums_ref[...]


def add_faces(kinds, place, adj, rows, x, blocks, modes=None, sums=None, first=False, count=0, tile=512):
    order, cases = x.shape
    last, extra = modes is not None, sums is not None
    args = [place, adj, rows, in_hbm(x) if first else x] + [modes] * last + [sums] * extra
    args += in_vmem(blocks)
    specs = [VMEM] * len(args)
    specs[:2] = [SMEM, SMEM]
    specs[3] = HBM if first else VMEM
    outs = [shaped((order, cases))]
    if last:
        outs.append(shaped((modes.shape[0] + PAD * extra, cases)))
    if count:
        outs.append(shaped((len(kinds) * rows.shape[1], 2 * len(kinds) * count), BF16))
    scratch = [pltpu.VMEM((len(kinds) * rows.shape[1], 2 * cases), BF16)]
    if first:
        scratch.append(pltpu.SemaphoreType.DMA(()))
    return call(
        functools.partial(add_kernel, kinds, len(blocks), first, last, extra, count, tile),
        "last_add" if last else "add",
        args,
        specs,
        outs,
        scratch,
        len(kinds) * order * order * cases,
        None if first else {3: 0},
    )


def extend_kernel(groups, tile, place_ref, adj_ref, rows_ref, contact_ref, op_ref, modes_source, *refs):
    parts, refs = refs[: len(groups)], refs[len(groups) :]
    w_high, w_low, weight_ref, clamp_ref, held, modes_ref, sems = refs
    copy = pltpu.make_async_copy(op_ref, held, sems.at[0])
    modes_copy = pltpu.make_async_copy(modes_source, modes_ref, sems.at[1])
    modes_copy.start()
    copy.start()
    modes_copy.wait()
    count = modes_ref.shape[0]

    def body(begin, rows):
        glued = jnp.zeros((tile, 1), F32)
        blocks = [jnp.transpose(modes_ref[:, rows])]
        for kinds, part in zip(groups, parts):
            faces = faces_of(kinds, place_ref)
            ones = placed_rows(faces, rows_ref, begin, tile)
            for face, one in zip(faces, ones):
                glued += adj_ref[face].astype(F32) * jnp.sum(one, axis=1, keepdims=True)
            near = dot(jnp.concatenate([one.astype(BF16) for one in ones], axis=1), part[...])
            for k in range(len(faces)):
                lane = 2 * k * count
                blocks.append(near[:, lane : lane + count] + near[:, lane + count : lane + 2 * count])
        row_free = 1.0 - glued
        weight_ref[rows] = 0.5 + 0.5 * row_free
        contact = column_of(contact_ref[:, rows].astype(F32))
        clamp_ref[rows] = jnp.where(contact * row_free > 0.5, 1.0, 0.0)
        high, low = parts_of(jnp.concatenate(blocks, axis=1))
        w_high[rows] = high
        w_low[rows] = low

    over_tiles(held.shape[0], tile, UNROLL["extend"], body)
    copy.wait()


def extend(groups, place, adj, rows, contact, op, modes, parts, tile=512):
    order, count = op.shape[0], modes.shape[0]
    args = [place, adj, rows, contact, in_hbm(op), in_hbm(modes), *parts]
    w, column = shaped((order, 5 * count), BF16), shaped((order, 1))
    return call(
        functools.partial(extend_kernel, groups, tile),
        "extend",
        args,
        [SMEM, SMEM, VMEM, VMEM, HBM, HBM] + [VMEM] * len(parts),
        [w, w, column, column, shaped(op.shape, op.dtype)],
        [pltpu.VMEM(modes.shape, modes.dtype), pltpu.SemaphoreType.DMA((2,))],
        2 * order * order * 8 * count,
    )


def coarse_kernel(offsets, extra, grid_rows, place_ref, *refs):
    inverse_refs, refs = refs[:grid_rows], refs[grid_rows:]
    pieces = refs[: len(offsets)]
    outs = refs[len(offsets) : len(offsets) + grid_rows]
    coef, amounts = refs[len(offsets) + grid_rows :]
    row, col = place_ref[0], place_ref[1]
    count = inverse_refs[0].shape[1] // 3
    tall = count + extra
    sums = None
    for piece, inside in zip(pieces, offsets):
        for k, offset in enumerate(inside):
            begin = pl.multiple_of((col ^ offset) * count, count)
            coef[pl.ds(begin, count)] = piece[k * tall : k * tall + count]
            if extra:
                term = piece[k * tall + count : (k + 1) * tall]
                sums = term if sums is None else sums + term
    tiles = inverse_refs[0].shape[0]
    inverse = [jnp.concatenate([ref[k] for k in range(tiles)], axis=1) for ref in inverse_refs]
    inverse = parts_of(jnp.concatenate(inverse, axis=0))
    amounts[...] = dot3(inverse, parts_of(coef[...])).reshape(amounts.shape)
    odd = col % 2
    for j in range(grid_rows):
        target = row ^ j
        cross = jnp.clip(target - 1 + 2 * (target % 2), 0, grid_rows - 1) ^ row
        order = (j * 3 + 1, j * 3 + 2 - 2 * odd, j * 3 + 2 * odd, (j ^ 1) * 3 + 1, cross * 3 + 1)
        for k, source in enumerate(order):
            outs[j][k * count : (k + 1) * count] = amounts[source]
        if extra:
            outs[j][5 * count :] = sums


def coarse(place, inverse, pieces, offsets, extra):
    grid_rows = len(inverse)
    tiles, three, width = inverse[0].shape
    count = three // 3
    cases = pieces[0].shape[1]
    args = [place, *in_vmem(inverse), *in_vmem(pieces)]
    return call(
        functools.partial(coarse_kernel, offsets, extra, grid_rows),
        "coarse",
        args,
        [SMEM] + [VMEM] * (len(args) - 1),
        [shaped((5 * count + extra, cases))] * grid_rows,
        [pltpu.VMEM((tiles * width, cases), F32), pltpu.VMEM((grid_rows * 3, count, cases), F32)],
        6 * grid_rows * three * tiles * width * cases,
    )


def first_kernel(tile, op_ref, s_ref, w_high, w_low, clamp_ref, *refs):
    *part_refs, d_ref, v_ref, field = refs
    order, cases = s_ref.shape
    amount = parts_of(total_of(part_refs))


    def prepare(_, rows):
        d = s_ref[rows] - dot3((w_high[rows], w_low[rows]), amount)
        d_ref[rows] = d
        h = jnp.where(clamp_ref[rows] > 0.5, jnp.maximum(-d, 0.0), -d)
        high, low = parts_of(h)
        field[rows, :cases] = high
        field[rows, cases:] = low

    def body(_, rows):
        got = dot(op_ref[rows], field[...])
        v_ref[rows] = got[:, :cases] + got[:, cases:]

    over_tiles(order, tile, UNROLL["prepare"], prepare)
    over_tiles(order, tile, UNROLL["first"], body)


def first(op, s, w, clamp, amounts, tile=512):
    order, cases = s.shape
    args = [op, s, *w, clamp, *in_vmem(amounts)]
    return call(
        functools.partial(first_kernel, tile),
        "first",
        args,
        [VMEM] * len(args),
        [shaped((order, cases))] * 2,
        [pltpu.VMEM((order, 2 * cases), BF16)],
        4 * order * order * cases,
        {1: 0},
    )


def add_sums(sums_ref, tile, op_ref, d_ref, weight_ref, field):
    sums_ref[...] = jnp.zeros_like(sums_ref)


    def body(_, rows):
        operated = dot(op_ref[rows], field[...])
        d = d_ref[rows]
        sums_ref[0:1] += jnp.sum(weight_ref[rows] * d * d, axis=0, keepdims=True)
        sums_ref[1:2] += jnp.sum(d * operated, axis=0, keepdims=True)

    over_tiles(d_ref.shape[0], tile, UNROLL["sums"], body)


def sums_kernel(tile, op_ref, d_ref, weight_ref, sums_ref, field):
    field[...] = d_ref[...].astype(BF16)
    add_sums(sums_ref, tile, op_ref, d_ref, weight_ref, field)


def step_sums(op, d, weight, tile=512):
    order, cases = d.shape
    return call(
        functools.partial(sums_kernel, tile),
        "step_sums",
        [op, d, weight],
        [VMEM] * 3,
        [shaped((PAD, cases))],
        [pltpu.VMEM((order, cases), BF16)],
        2 * order * order * cases,
    )[0]


def second_kernel(tile, op_ref, s_ref, d0_ref, w_high, w_low, weight_ref, *refs):
    *part_refs, d_ref, sums_ref, step_ref, field = refs
    order, cases = s_ref.shape
    wide = w_high.shape[1]
    amount = total_of(part_refs)
    length = amount[wide : wide + 1] / amount[wide + 1 : wide + 2]
    step_ref[...] = jnp.broadcast_to(length, step_ref.shape)
    amount = parts_of(amount[:wide])


    def prepare(_, rows):
        q = s_ref[rows] - dot3((w_high[rows], w_low[rows]), amount)
        d = length * q + d0_ref[rows]
        d_ref[rows] = d
        field[rows] = d.astype(BF16)

    over_tiles(order, tile, UNROLL["prepare"], prepare)
    add_sums(sums_ref, tile, op_ref, d_ref, weight_ref, field)


def second(op, s, d0, w, weight, amounts, tile=512):
    order, cases = s.shape
    args = [op, s, d0, *w, weight, *in_vmem(amounts)]
    return call(
        functools.partial(second_kernel, tile),
        "second",
        args,
        [VMEM] * len(args),
        [shaped((order, cases)), shaped((PAD, cases)), shaped((PAD, cases))],
        [pltpu.VMEM((order, cases), BF16)],
        2 * order * order * cases,
        {1: 0},
    )


def finish_kernel(d0_ref, d1_ref, clamp_ref, step_ref, *refs):
    *sum_refs, out_ref = refs
    sums = total_of(sum_refs)
    low = jnp.where(clamp_ref[...] > 0.5, 0.0, -jnp.inf)
    once = jnp.maximum(-(step_ref[0:1] * d0_ref[...]), low)
    length = sums[0:1] / sums[1:2]
    out_ref[...] = jnp.maximum(once - length * d1_ref[...], low)


def finish(d0, d1, clamp, step, sums, tile=512):
    order, cases = d0.shape
    block = pl.BlockSpec((tile, cases), lambda i: (i, 0))
    small = pl.BlockSpec((PAD, cases), lambda i: (0, 0))
    return pl.pallas_call(
        finish_kernel,
        grid=(order // tile,),
        in_specs=[block, block, pl.BlockSpec((tile, 1), lambda i: (i, 0))] + [small] * (1 + len(sums)),
        out_specs=block,
        out_shape=jax.ShapeDtypeStruct((order, cases), F32),
        compiler_params=pltpu.CompilerParams(vmem_limit_bytes=GRANT),
        cost_estimate=pl.CostEstimate(flops=4 * order * cases, bytes_accessed=12 * order * cases, transcendentals=0),
        name="finish",
    )(d0, d1, clamp, step, *sums)


def send(x, axis, target):
    size = lax.axis_size(axis)
    pairs = [(i, target(i)) for i in range(size)]
    return lax.ppermute(x, axis, [(i, j) for i, j in pairs if j is not None and 0 <= j < size])


def swap(x, axis, bits):
    return send(x, axis, lambda i: i ^ bits)


def other_side(i):
    return i + 1 if i % 2 else i - 1


def row_exchange(place, *sends):
    size = lax.axis_size("row")
    if not splits(size):
        got = [swap(sends[0], "row", 1), send(sends[1], "row", other_side)]
        return got, got
    both, other, last = sends
    both = swap(both, "row", 1)
    other = send(other, "row", lambda i: i ^ 2 if i in (1, 2) else None)
    to_pair, to_far = relay(place, both, other, last)
    got_last = swap(to_pair, "row", 1)
    got_other = send(to_far, "row", lambda i: i ^ 2 if i in (0, 3) else None)
    return [both, other], [both, got_last, got_other]


def col_exchange(pair, cross):
    return swap(pair, "col", 1), send(cross, "col", other_side)


def gather_cols(block):
    size = lax.axis_size("col")
    far = list(range(2, size, 2))
    pieces = [block] + [swap(block, "col", j) for j in far]
    held = jnp.concatenate(pieces, axis=0)
    known = [0] + far
    return pieces + [swap(held, "col", 1)], [[j] for j in known] + [[j ^ 1 for j in known]]


def coarse_amounts(place, inverse, block, extra):
    pieces, offsets = gather_cols(block)
    sends = coarse(place, inverse, pieces, offsets, extra)
    return [sends[0]] + [swap(sends[j], "row", j) for j in range(1, lax.axis_size("row"))], sends[0]


def by_row(three):
    grid_rows = lax.axis_size("row")
    tiles = three.shape[0] // grid_rows
    row = lax.axis_index("row")
    return [lax.dynamic_slice_in_dim(three, (row ^ j) * tiles, tiles, 0) for j in range(grid_rows)]


def spread_rows(picked):
    return [picked[0]] + [swap(picked[j], "row", j) for j in range(1, len(picked))]


def after(x, *others):
    return lax.optimization_barrier((x, *others))[0]


def after_all(arrays, others):
    return lax.optimization_barrier((*arrays, *others))[: len(arrays)]


COLS = ((2, False), (2, True))
ROWS = ((0, False), (0, True))


def per_device(local_ops, loads, modes, coarse_inverse, face_rows, adjacency, contact):
    op, load, mode = local_ops[0, 0], loads[0, 0], modes[0, 0]
    rows, adj = face_rows[0, 0], adjacency[0, 0]
    touch = contact[0, 0][None]
    count = mode.shape[0]
    place = jnp.stack([lax.axis_index("row"), lax.axis_index("col")]).astype(jnp.int32)

    *row_sends, x_parts, m_parts, rows, three = to_faces(0, place, rows, load, mode, coarse_inverse)
    way, row_got = row_exchange(place, *row_sends)
    col_sends = to_faces(2, place, rows, x_parts, m_parts)
    col_got = col_exchange(*after_all(col_sends, way))
    picked = by_row(lax.all_to_all(after(three, *col_sends), "col", 0, 0, tiled=True))
    inverse = spread_rows(picked)
    part, m_cols = add_faces(COLS, place, adj, rows, load, col_got, first=True, count=count)
    s0, coef, m_rows = add_faces(ROWS, after(place, *picked), adj, rows, part, row_got, modes=mode, count=count)
    amounts, own = coarse_amounts(place, inverse, after(coef, *inverse), 0)
    w_high, w_low, weight, clamp, op = extend(
        (COLS, ROWS), after(place, own), adj, rows, touch, op, mode, (m_cols, m_rows)
    )
    w = (w_high, w_low)
    d0, v = first(op, s0, w, clamp, amounts)

    *row_sends, x_parts = to_faces(0, place, rows, v)
    way, row_got = row_exchange(place, *row_sends)
    col_sends = to_faces(2, place, rows, x_parts)
    col_got = [swap(col_sends[0], "col", 1), send(after(col_sends[1], way[1]), "col", other_side)]
    sums = step_sums(op, d0, after(weight, *way, col_got[0]))
    (part,) = add_faces(COLS, place, adj, rows, v, col_got)
    s1, coef = add_faces(ROWS, place, adj, rows, part, row_got, mode, sums)
    amounts, _ = coarse_amounts(place, inverse, coef, PAD)
    d1, sums, step = second(op, s1, d0, w, weight, amounts)

    grid_rows, grid_cols = lax.axis_size("row"), lax.axis_size("col")
    sums = sum((swap(sums, "row", j) for j in range(1, grid_rows)), sums)
    sums = sum((swap(sums, "col", j) for j in range(2, grid_cols, 2)), sums)
    return finish(d0, d1, clamp, step, [sums, swap(sums, "col", 1)])[None, None]


def solution(mesh):
    placed = (
        P("row", "col", None, None),
        P("row", "col", None, None),
        P("row", "col", None, None),
        P("row", "col"),
        P("row", "col", None, None),
        P("row", "col", None),
        P("row", "col", None),
    )
    return jax.shard_map(
        per_device,
        mesh=mesh,
        in_specs=placed,
        out_specs=P("row", "col", None, None),
        check_vma=False,
    )
```
